128 devices in a mesh: pipe: 8 (over x, y_hi), expert: 16 (over y_lo, z, core).
Axes of the slice: x: 4, y: 4 (y_hi: 2, y_lo: 2; y = y_hi * 2 + y_lo), z: 4, core: 2. Of those that a mesh axis runs over, the one named last changes fastest.
Arguments:
- acts: bfloat16 [8, 2048, 3584], P('pipe', 'expert'), may hold values from -6 to 6
- grad_out: bfloat16 [8, 2048, 3584], P('pipe', 'expert'), may hold values from -6 to 6
- expert_ids: int32 [8, 2048, 2], P('pipe', 'expert'), may hold values from 0 to 7, all different within a row; in each aligned block of 64 rows (0 to 63, 64 to 127, ..., all dimensions but the last counted through in order) at most 24 rows name the same one
- route_weights: float32 [8, 2048, 2], P('pipe', 'expert'), may hold values from 0.1 to 1
- w_gate: bfloat16 [8, 3584, 8192], P('pipe', None, 'expert'), may hold values from -0.09375 to 0.09375
- w_up: bfloat16 [8, 3584, 8192], P('pipe', None, 'expert'), may hold values from -0.09375 to 0.09375
- w_down: bfloat16 [8, 8192, 3584], P('pipe', 'expert'), may hold values from -0.1875 to 0.1875
Outputs:
- out_acts: bfloat16 [8, 2048, 3584], P('pipe', 'expert')
- grad_acts: bfloat16 [8, 2048, 3584], P('pipe', 'expert')
- grad_gate: bfloat16 [8, 3584, 4096], P('pipe', None, 'expert')
- grad_up: bfloat16 [8, 3584, 4096], P('pipe', None, 'expert')
- grad_down: bfloat16 [8, 4096, 3584], P('pipe', 'expert')
The draws below stay inside these ranges and needn't reach their ends.
Inputs may be any that keep to these rules, and one draw needn't show every extreme that they name: `expert_ids`: in each aligned block of 64 rows of one rank (one micro-batch of one device), no expert is named by more than 24 rows; the 2 experts of a row differ.
All inputs are finite; a program needn't handle non-finite values.
Results may differ from the reference program's by a relative error of at most 0.0072.
Values may be sent and summed in bfloat16 or wider, within the bound.
A program may use at most 192 MiB of HBM per device.

```python
import math
import jax
import jax.numpy as jnp
import numpy as np
from jax import lax

D = 3584
FF = 1024
TOPK = 2
MB = 2
TOK_MB = 64
NEXP = 8
FF_DEV = 512
CAP = 24
TOKENS = 2048
N_PIPE = 8
N_EXPERT = 16


def shard_levels(stream_key, dims, cuts, least, largest):
    factor_of, own = 1.0, jax.random.fold_in(stream_key, 6)
    for axis_at, blocks in cuts:
        draws = jnp.exp(jax.random.uniform(jax.random.fold_in(own, axis_at), (blocks,), jnp.float32, least / len(cuts), largest / len(cuts)))
        factor_of = factor_of * jnp.repeat(draws, dims[axis_at] // blocks).reshape([-1 if axis == axis_at else 1 for axis in range(len(dims))])
    return factor_of


def shared_out(stream_key, own, number, rows, count, top, limit, lean):
    ranking = jax.random.permutation(stream_key, count)
    packed, ordinary = portions_of(count, rows * top, limit, lean, True), portions_of(count, rows * top, limit, lean, False)
    places = jnp.arange(count)

    def named(sizes, turn):
        used = int((sizes > 0).sum())
        fixed = max(1, used // 4)
        moved = fixed + (places - fixed + turn * (used - fixed)) % max(1, count - fixed)
        return jnp.zeros((count,), jnp.int32).at[ranking[jnp.where(places < fixed, places, moved)]].set(jnp.asarray(sizes, jnp.int32))

    sizes = jnp.where(number % 4 == 0, named(packed, number // 4), named(ordinary, number - number // 4 - 1))
    mixed = jax.random.permutation(jax.random.fold_in(own, 3), count)
    donor, sink = mixed[0:count // 2 * 2:2], mixed[1:count // 2 * 2:2]
    slack = jnp.minimum(sizes[donor] - 1, limit - sizes[sink]) // 2
    slack = jnp.where((donor == ranking[0]) | (sink == ranking[0]) | (sizes[sink] == 0), 0, jnp.maximum(slack, 0))
    moved = jax.random.randint(jax.random.fold_in(own, 4), (count // 2,), 0, 1 << 20) % (slack + 1)
    sizes = sizes.at[donor].add(-moved).at[sink].add(moved)
    items = jnp.searchsorted(jnp.cumsum(sizes), jnp.arange(rows * top), side="right").astype(jnp.int32)
    listing = items.reshape(top, rows).T
    listing = listing[jax.random.permutation(jax.random.fold_in(own, 1), rows)]
    turn = jax.random.randint(jax.random.fold_in(own, 2), (rows, 1), 0, top)
    return jnp.take_along_axis(listing, (jnp.arange(top)[None, :] + turn) % top, axis=1)


def portions_of(number_of, total, limit, lean, full):
    portions = [(1 << 20) // math.isqrt(standing ** lean) + 1 for standing in range(1, number_of + 1)]
    largest = limit if full else min(limit, max(-(-total // number_of), total * portions[0] // sum(portions)))
    least = 1 if total - largest >= number_of - 1 else 0
    counts, surplus = [largest] + [least] * (number_of - 1), total - largest - least * (number_of - 1)
    while surplus > 0:
        movable = [i for i in range(1, number_of) if counts[i] < largest] or [i for i in range(1, number_of) if counts[i] < limit]
        mass, remaining = sum([portions[i] for i in movable]), surplus
        for i in movable:
            more = min(limit - counts[i], max(1, remaining * portions[i] // mass), surplus)
            counts[i] = counts[i] + more
            surplus = surplus - more
    return np.array(counts)


def gaussian(key, extent, scale, bound, shards=(), kind=jnp.bfloat16):
    gain = shard_levels(key, extent, shards, -0.22, 0.18) if shards else 1.0
    array = jax.random.normal(key, extent, jnp.float32) * scale * gain
    return jnp.minimum(jnp.maximum(array, -bound), bound).astype(kind)


def setup_inputs(seed: int = 0) -> dict:
    keys = jax.random.split(jax.random.key(seed), 8)
    acts = gaussian(keys[0], (N_PIPE, TOKENS, D), 1.0, 6.0, ((0, 8), (1, 16)))
    grad_out = gaussian(keys[1], (N_PIPE, TOKENS, D), 1.0, 6.0, ((0, 8), (1, 16)))
    expert_ids_keys = jax.random.split(jax.random.fold_in(keys[2], 1), N_PIPE * TOKENS // TOK_MB)
    expert_ids_turns = jax.random.permutation(jax.random.fold_in(keys[2], 3), N_PIPE * TOKENS // TOK_MB)
    expert_ids = jax.vmap(lambda own, number: shared_out(jax.random.fold_in(keys[2], 2), own, number, TOK_MB, NEXP, TOPK, CAP, 2))(expert_ids_keys, expert_ids_turns).reshape((N_PIPE, TOKENS, TOPK))
    route_weights = jnp.clip(0.1 + 0.9 * jax.random.uniform(keys[3], (N_PIPE, TOKENS, TOPK), jnp.float32) ** shard_levels(keys[3], (N_PIPE, TOKENS, TOPK), ((0, 8), (1, 16)), -0.2, 0.2), 0.1, 1.0)
    w_gate = gaussian(keys[4], (N_PIPE, D, N_EXPERT * FF_DEV), D ** -0.5, 0.09375, ((0, 8), (2, 16)))
    w_up = gaussian(keys[5], (N_PIPE, D, N_EXPERT * FF_DEV), D ** -0.5, 0.09375, ((0, 8), (2, 16)))
    w_down = gaussian(keys[6], (N_PIPE, N_EXPERT * FF_DEV, D), FF ** -0.5, 0.1875, ((0, 8), (1, 16)))
    return {"acts": acts, "grad_out": grad_out, "expert_ids": expert_ids, "route_weights": route_weights, "w_gate": w_gate, "w_up": w_up, "w_down": w_down}


def expert_half(rows_in, rows_grad, gate_weight, up_weight, down_weight):
    pre_gate = jnp.dot(rows_in, gate_weight, preferred_element_type=jnp.float32)
    pre_up = jnp.dot(rows_in, up_weight, preferred_element_type=jnp.float32)
    sigma = jax.nn.sigmoid(pre_gate)
    active = pre_gate * sigma
    hidden = (active * pre_up).astype(jnp.bfloat16)
    part_out = jnp.dot(hidden, down_weight, preferred_element_type=jnp.float32).astype(jnp.bfloat16)
    hidden_grad = lax.dot_general(rows_grad, down_weight, (((1,), (1,)), ((), ())), preferred_element_type=jnp.float32)
    gate_grad = (hidden_grad * pre_up * sigma * (1.0 + pre_gate * (1.0 - sigma))).astype(jnp.bfloat16)
    up_grad = (hidden_grad * active).astype(jnp.bfloat16)
    part_input = lax.dot_general(gate_grad, gate_weight, (((1,), (1,)), ((), ())), preferred_element_type=jnp.float32)
    part_input = part_input + lax.dot_general(up_grad, up_weight, (((1,), (1,)), ((), ())), preferred_element_type=jnp.float32)
    grad_gate = lax.dot_general(rows_in, gate_grad, (((0,), (0,)), ((), ())), preferred_element_type=jnp.float32)
    grad_up = lax.dot_general(rows_in, up_grad, (((0,), (0,)), ((), ())), preferred_element_type=jnp.float32)
    grad_down = lax.dot_general(hidden, rows_grad, (((0,), (0,)), ((), ())), preferred_element_type=jnp.float32)
    return part_out, part_input.astype(jnp.bfloat16), grad_gate, grad_up, grad_down


def keep_halves(summed, axis_pos):
    if axis_pos == 2:
        shaped = summed.reshape(N_PIPE, D, N_EXPERT, 2, FF_DEV // 2)
        lower = shaped[: N_PIPE // 2, :, :, 0]
        upper = shaped[N_PIPE // 2:, :, :, 1]
        return jnp.concatenate([lower, upper], axis=0).reshape(N_PIPE, D, N_EXPERT * FF_DEV // 2)
    shaped = summed.reshape(N_PIPE, N_EXPERT, 2, FF_DEV // 2, D)
    lower = shaped[: N_PIPE // 2, :, 0]
    upper = shaped[N_PIPE // 2:, :, 1]
    return jnp.concatenate([lower, upper], axis=0).reshape(N_PIPE, N_EXPERT * FF_DEV // 2, D)


def mirror_sum(local):
    return (local.astype(jnp.float32) + local[::-1].astype(jnp.float32)).astype(jnp.bfloat16)


def reference(acts, grad_out, expert_ids, route_weights, w_gate, w_up, w_down):
    total_slots = N_EXPERT * MB * CAP
    positions = jnp.arange(total_slots, dtype=jnp.int32)
    zero_value = jnp.zeros((), jnp.bfloat16)
    out_list = []
    input_list = []
    gate_list = []
    up_list = []
    down_list = []
    for rank in range(N_PIPE):
        token_rows = acts[rank]
        choice_ids = expert_ids[rank].reshape(-1)
        choice_gain = route_weights[rank].reshape(-1)
        scaled_grad = (route_weights[rank][:, :, None] * grad_out[rank][:, None, :].astype(jnp.float32)).astype(jnp.bfloat16).reshape(-1, D)
        out_acc = jnp.zeros((TOKENS, D), jnp.float32)
        input_acc = jnp.zeros((TOKENS, D), jnp.float32)
        gate_cols = []
        up_cols = []
        down_rows = []
        for expert in range(NEXP):
            chosen = choice_ids == expert
            found = jnp.nonzero(chosen, size=total_slots, fill_value=0)[0].astype(jnp.int32)
            number = jnp.sum(chosen.astype(jnp.int32))
            live = positions < number
            row_index = (found // TOPK).astype(jnp.int32)
            rows_in = jnp.where(live[:, None], token_rows[row_index], zero_value)
            rows_grad = jnp.where(live[:, None], scaled_grad[found], zero_value)
            out_sum = jnp.zeros((total_slots, D), jnp.float32)
            input_sum = jnp.zeros((total_slots, D), jnp.float32)
            for half_index in range(2):
                start = (2 * expert + half_index) * FF_DEV
                part_out, part_input, grad_g, grad_u, grad_d = expert_half(
                    rows_in, rows_grad, w_gate[rank][:, start:start + FF_DEV],
                    w_up[rank][:, start:start + FF_DEV], w_down[rank][start:start + FF_DEV, :])
                out_sum = out_sum + part_out.astype(jnp.float32)
                input_sum = input_sum + part_input.astype(jnp.float32)
                gate_cols.append(grad_g)
                up_cols.append(grad_u)
                down_rows.append(grad_d)
            expert_out = out_sum.astype(jnp.bfloat16).astype(jnp.float32)
            expert_input = input_sum.astype(jnp.bfloat16).astype(jnp.float32)
            gains = jnp.where(live, choice_gain[found], jnp.zeros((), jnp.float32))
            out_acc = out_acc.at[row_index].add(gains[:, None] * expert_out)
            input_acc = input_acc.at[row_index].add(jnp.where(live[:, None], expert_input, jnp.zeros((), jnp.float32)))
        out_list.append(out_acc.astype(jnp.bfloat16))
        input_list.append(input_acc.astype(jnp.bfloat16))
        gate_list.append(jnp.concatenate(gate_cols, axis=1).astype(jnp.bfloat16))
        up_list.append(jnp.concatenate(up_cols, axis=1).astype(jnp.bfloat16))
        down_list.append(jnp.concatenate(down_rows, axis=0).astype(jnp.bfloat16))
    grad_gate = keep_halves(mirror_sum(jnp.stack(gate_list)), 2)
    grad_up = keep_halves(mirror_sum(jnp.stack(up_list)), 2)
    grad_down = keep_halves(mirror_sum(jnp.stack(down_list)), 1)
    return jnp.stack(out_list), jnp.stack(input_list), grad_gate, grad_up, grad_down
```

```python
import functools

import jax
import jax.numpy as jnp
from jax import lax
from jax.experimental import pallas as pl
from jax.experimental.pallas import tpu as pltpu
from jax.sharding import PartitionSpec as P

MESH = pl.DeviceIdType.MESH
CHIPS = 8
CAP = 48


def place():
    pipe = lax.axis_index("pipe")
    own = lax.axis_index("expert")
    return pipe, own, own // 8, (own // 2) % 4, own % 2


def chip_at(y, z, k, sign):
    return ((y + k // 4) % 2) * 4 + (z + 4 + sign * (k % 4)) % 4


def greet(pipe, own, y, z, core):
    barrier = pltpu.get_barrier_semaphore()
    for k in range(1, CHIPS):
        peer = chip_at(y, z, k, 1) * 2 + core
        pl.semaphore_signal(barrier, inc=1, device_id=(pipe, peer), device_id_type=MESH)
    sibling = own + 1 - 2 * core
    pl.semaphore_signal(barrier, inc=1, device_id=(pipe, sibling), device_id_type=MESH)
    pl.semaphore_wait(barrier, CHIPS)
    return sibling


def dispatch_kernel(
    tokens, grads, got_tokens, got_grads, send_sem, recv_sem, near_send, near_recv, own_sem
):
    pipe, own, y, z, core = place()
    chip = own // 2
    sibling = greet(pipe, own, y, z, core)
    arrays = ((tokens, got_tokens), (grads, got_grads))

    def far(a, k):
        source, target = arrays[a]
        dest = chip_at(y, z, k, 1)
        return pltpu.make_async_remote_copy(
            src_ref=source.at[dest],
            dst_ref=target.at[own],
            send_sem=send_sem.at[a, k],
            recv_sem=recv_sem.at[a, k],
            device_id=(pipe, dest * 2 + core),
            device_id_type=MESH,
        )

    def near(a, k):
        source, target = arrays[a]
        origin = chip_at(y, z, k, -1) * 2 + core
        return pltpu.make_async_remote_copy(
            src_ref=source.at[chip] if k == 0 else target.at[origin],
            dst_ref=target.at[origin],
            send_sem=near_send.at[a, k],
            recv_sem=near_recv.at[a, k],
            device_id=(pipe, sibling),
            device_id_type=MESH,
        )

    def stay(a):
        source, target = arrays[a]
        return pltpu.make_async_copy(source.at[chip], target.at[own], own_sem.at[a])

    for a in range(2):
        for k in (6, 2, 5, 7, 1, 3, 4):
            far(a, k).start()
        stay(a).start()
        near(a, 0).start()
    for a in range(2):
        for k in (4, 1, 3, 5, 7, 2, 6):
            far(a, k).wait_recv()
            near(a, k).start()
    for a in range(2):
        stay(a).wait()
        for k in range(CHIPS):
            near(a, k).wait()
            if k:
                far(a, k).wait_send()


def dispatch(tokens, grads):
    width = tokens.shape[-1]
    anywhere = pl.BlockSpec(memory_space=pl.ANY)
    dma = pltpu.SemaphoreType.DMA
    shape = jax.ShapeDtypeStruct((2 * CHIPS, CAP, width), tokens.dtype)
    return pl.pallas_call(
        dispatch_kernel,
        name="dispatch",
        out_shape=(shape, shape),
        in_specs=[anywhere] * 2,
        out_specs=(anywhere, anywhere),
        scratch_shapes=[dma((2, CHIPS))] * 4 + [dma((2,))],
        compiler_params=pltpu.CompilerParams(collective_id=1, has_side_effects=True),
    )(tokens, grads)


def return_kernel(
    out_part,
    input_part,
    back_out,
    back_input,
    halves,
    sums,
    mine,
    send_sem,
    recv_sem,
    near_send,
    near_recv,
    mine_sem,
    own_sem,
):
    pipe, own, y, z, core = place()
    chip = own // 2
    sibling = greet(pipe, own, y, z, core)
    arrays = ((out_part, back_out), (input_part, back_input))

    def near(a, k):
        there = chip_at(y, z, k, 1) * 2 + 1 - core
        return pltpu.make_async_remote_copy(
            src_ref=arrays[a][0].at[there],
            dst_ref=halves.at[a, k],
            send_sem=near_send.at[a, k],
            recv_sem=near_recv.at[a, k],
            device_id=(pipe, sibling),
            device_id_type=MESH,
        )

    def load(a, k):
        here = chip_at(y, z, k, 1) * 2 + core
        return pltpu.make_async_copy(arrays[a][0].at[here], mine.at[a, k], mine_sem.at[a, k])

    def far(a, k):
        return pltpu.make_async_remote_copy(
            src_ref=sums.at[a, k],
            dst_ref=arrays[a][1].at[chip],
            send_sem=send_sem.at[a, k],
            recv_sem=recv_sem.at[a, k],
            device_id=(pipe, chip_at(y, z, k, 1) * 2 + core),
            device_id_type=MESH,
        )

    def stay(a):
        return pltpu.make_async_copy(sums.at[a, 0], arrays[a][1].at[chip], own_sem.at[a])

    order = (6, 2, 5, 7, 1, 3, 4, 0)
    for a in range(2):
        for k in order:
            near(a, k).start()
            load(a, k).start()
    for a in range(2):
        for k in order:
            load(a, k).wait()
            near(a, k).wait_recv()
            total = halves[a, k].astype(jnp.float32) + mine[a, k].astype(jnp.float32)
            sums[a, k] = total.astype(jnp.bfloat16)
            if k:
                far(a, k).start()
            else:
                stay(a).start()
    for a in range(2):
        stay(a).wait()
        for k in range(CHIPS):
            near(a, k).wait_send()
            if k:
                far(a, k).wait()


def give_back(out_part, input_part):
    width = out_part.shape[-1]
    anywhere = pl.BlockSpec(memory_space=pl.ANY)
    dma = pltpu.SemaphoreType.DMA
    shape = jax.ShapeDtypeStruct((CHIPS, CAP, width), out_part.dtype)
    block = pltpu.VMEM((2, CHIPS, CAP, width), out_part.dtype)
    return pl.pallas_call(
        return_kernel,
        name="give_back",
        out_shape=(shape, shape),
        in_specs=[anywhere] * 2,
        out_specs=(anywhere, anywhere),
        scratch_shapes=[block] * 3 + [dma((2, CHIPS))] * 5 + [dma((2,))],
        compiler_params=pltpu.CompilerParams(
            collective_id=2, has_side_effects=True, vmem_limit_bytes=40 << 20
        ),
    )(out_part, input_part)


def split_gain(gain):
    high = gain.astype(jnp.bfloat16)
    return high, (gain - high.astype(jnp.float32)).astype(jnp.bfloat16)


def dot(a, b, contract):
    return lax.dot_general(a, b, ((contract[:1], contract[1:]), ((), ())), preferred_element_type=jnp.float32)


def on_device(acts, grad_out, expert_ids, route_weights, w_gate, w_up, w_down):
    tokens, grads, ids, gain = acts[0], grad_out[0], expert_ids[0], route_weights[0]
    gate_weight, up_weight, down_weight = w_gate[0], w_up[0], w_down[0]
    count, top = ids.shape
    width = tokens.shape[1]
    units = gate_weight.shape[1]

    flat = ids.reshape(-1)
    member = (flat[:, None] == jnp.arange(CHIPS, dtype=jnp.int32)[None, :]).astype(jnp.bfloat16)
    before = jnp.tril(jnp.ones((count * top, count * top), jnp.bfloat16), -1)
    rank = jnp.sum(dot(before, member, (1, 0)) * member.astype(jnp.float32), axis=1)
    slot = (flat * CAP + rank.astype(jnp.int32)).reshape(count, top)
    hits = (slot[:, :, None] == jnp.arange(CHIPS * CAP, dtype=jnp.int32)).astype(jnp.float32)
    placing = jnp.sum(hits, axis=1).astype(jnp.bfloat16)
    high, low = split_gain(jnp.sum(hits * gain[:, :, None], axis=1))

    slot_tokens = dot(placing, tokens, (0, 0)).astype(jnp.bfloat16)
    slot_grads = (dot(high, grads, (0, 0)) + dot(low, grads, (0, 0))).astype(jnp.bfloat16)
    rows_in, rows_grad = dispatch(
        slot_tokens.reshape(CHIPS, CAP, width), slot_grads.reshape(CHIPS, CAP, width)
    )
    rows_in = rows_in.reshape(2 * CHIPS * CAP, width)
    rows_grad = rows_grad.reshape(2 * CHIPS * CAP, width)

    pre_gate = dot(rows_in, gate_weight, (1, 0))
    pre_up = dot(rows_in, up_weight, (1, 0))
    hidden_grad = dot(rows_grad, down_weight, (1, 1))
    sigma = jax.nn.sigmoid(pre_gate)
    active = pre_gate * sigma
    hidden = (active * pre_up).astype(jnp.bfloat16)
    gate_grad = (hidden_grad * pre_up * sigma * (1.0 + pre_gate * (1.0 - sigma))).astype(
        jnp.bfloat16
    )
    up_grad = (hidden_grad * active).astype(jnp.bfloat16)

    pipe = lax.axis_index("pipe")
    ranks = lax.axis_size("pipe")
    half = units // 2
    kept = (pipe >= ranks // 2).astype(jnp.int32) * half
    mirror = [(p, ranks - 1 - p) for p in range(ranks)]

    def cut(array, start):
        return lax.dynamic_slice_in_dim(array, start, half, 1)

    gave = [
        lax.ppermute(part.astype(jnp.bfloat16), "pipe", mirror)
        for part in (
            dot(rows_in, cut(gate_grad, half - kept), (0, 0)),
            dot(rows_in, cut(up_grad, half - kept), (0, 0)),
            dot(cut(hidden, half - kept), rows_grad, (0, 0)),
        )
    ]

    out_part = dot(hidden, down_weight, (1, 0)).astype(jnp.bfloat16)
    input_part = (dot(gate_grad, gate_weight, (1, 1)) + dot(up_grad, up_weight, (1, 1))).astype(
        jnp.bfloat16
    )
    back_out, back_input = give_back(
        out_part.reshape(2 * CHIPS, CAP, width), input_part.reshape(2 * CHIPS, CAP, width)
    )
    back_out = back_out.reshape(CHIPS * CAP, width)
    back_input = back_input.reshape(CHIPS * CAP, width)
    out_acts = (dot(high, back_out, (1, 0)) + dot(low, back_out, (1, 0))).astype(jnp.bfloat16)
    grad_acts = dot(placing, back_input, (1, 0)).astype(jnp.bfloat16)

    kept_parts = (
        dot(rows_in, cut(gate_grad, kept), (0, 0)),
        dot(rows_in, cut(up_grad, kept), (0, 0)),
        dot(cut(hidden, kept), rows_grad, (0, 0)),
    )
    sums = [
        (part.astype(jnp.bfloat16).astype(jnp.float32) + other.astype(jnp.float32)).astype(jnp.bfloat16)[None]
        for part, other in zip(kept_parts, gave)
    ]
    return (out_acts[None], grad_acts[None], *sums)


def solution(mesh):
    rows = P("pipe", "expert", None)
    columns = P("pipe", None, "expert")
    return jax.shard_map(
        on_device,
        mesh=mesh,
        in_specs=(rows, rows, rows, rows, columns, columns, rows),
        out_specs=(rows, rows, columns, columns, rows),
        check_vma=False,
    )
```

```python
import functools

import jax
import jax.numpy as jnp
from jax import lax
from jax.experimental import pallas as pl
from jax.experimental.pallas import tpu as pltpu
from jax.sharding import PartitionSpec as P

MESH = pl.DeviceIdType.MESH
CHIPS = 8
CAP = 48


def place():
    pipe = lax.axis_index("pipe")
    own = lax.axis_index("expert")
    return pipe, own, own // 8, (own // 2) % 4, own % 2


def chip_at(y, z, k, sign):
    return ((y + k // 4) % 2) * 4 + (z + 4 + sign * (k % 4)) % 4


def split_gain(gain):
    high = lax.reduce_precision(gain, exponent_bits=8, mantissa_bits=7)
    low = lax.reduce_precision(gain - high, exponent_bits=8, mantissa_bits=7)
    return high.astype(jnp.bfloat16), low.astype(jnp.bfloat16)


def dot(a, b, contract):
    dims = ((contract[:1], contract[1:]), ((), ()))
    return lax.dot_general(a, b, dims, preferred_element_type=jnp.float32)


def forward_kernel(
    tokens,
    grads,
    packing,
    away_weight,
    w_gate,
    w_up,
    w_down,
    got_in,
    got_grad,
    relay_weight,
    hidden,
    gate_grad,
    up_grad,
    out_part,
    slots,
    rows,
    gate,
    up,
    down,
    pre,
    out,
    send_sem,
    recv_sem,
    near_send,
    near_recv,
    load_sem,
    keep_sem,
    out_sem,
    away_sem,
):
    pipe, own, y, z, core = place()
    chip = own // 2
    sibling = own + 1 - 2 * core
    width = tokens.shape[1]
    units = hidden.shape[1]
    step = width // 7
    group = CHIPS * CAP

    barrier = pltpu.get_barrier_semaphore()
    for k in range(1, CHIPS):
        peer = chip_at(y, z, k, 1) * 2 + core
        pl.semaphore_signal(barrier, inc=1, device_id=(pipe, peer), device_id_type=MESH)
    pl.semaphore_signal(barrier, inc=1, device_id=(pipe, sibling), device_id_type=MESH)

    loads = [
        pltpu.make_async_copy(source, target, load_sem.at[i])
        for i, (source, target) in enumerate(((w_gate, gate), (w_up, up), (w_down, down)))
    ]

    def far(a, k):
        dest = chip_at(y, z, k, 1)
        return pltpu.make_async_remote_copy(
            src_ref=slots.at[a, dest],
            dst_ref=rows.at[a, own],
            send_sem=send_sem.at[a, k],
            recv_sem=recv_sem.at[a, k],
            device_id=(pipe, dest * 2 + core),
            device_id_type=MESH,
        )

    def near(a, k):
        origin = chip_at(y, z, k, -1) * 2 + core
        return pltpu.make_async_remote_copy(
            src_ref=slots.at[a, chip] if k == 0 else rows.at[a, origin],
            dst_ref=rows.at[a, origin],
            send_sem=near_send.at[a, k],
            recv_sem=near_recv.at[a, k],
            device_id=(pipe, sibling),
            device_id_type=MESH,
        )

    away = pltpu.make_async_remote_copy(
        src_ref=away_weight,
        dst_ref=relay_weight,
        send_sem=away_sem.at[0],
        recv_sem=away_sem.at[1],
        device_id=(pipe, (own + CHIPS) % (2 * CHIPS)),
        device_id_type=MESH,
    )
    keeps = [
        pltpu.make_async_copy(rows.at[a], target, keep_sem.at[a])
        for a, target in enumerate((got_in, got_grad))
    ]

    def pack(a):
        def tile(j, carry):
            columns = pl.ds(pl.multiple_of(j * step, step), step)
            if a == 0:
                total = dot(packing[2], tokens[:, columns], (1, 0))
            else:
                part = grads[:, columns]
                total = dot(packing[0], part, (1, 0)) + dot(packing[1], part, (1, 0))
            slots[a, :, :, columns] = total.astype(jnp.bfloat16).reshape(CHIPS, CAP, step)
            return carry

        lax.fori_loop(0, 7, tile, 0)

    def send(a):
        for k in (6, 2, 5, 7, 1, 3, 4):
            far(a, k).start()
        near(a, 0).start()
        rows[a, own] = slots[a, chip]

    def receive(a):
        for k in (4, 1, 3, 5, 7, 2, 6):
            far(a, k).wait_recv()
            near(a, k).start()
        for k in range(CHIPS):
            near(a, k).wait_recv()
        keeps[a].start()

    pack(0)
    pl.semaphore_wait(barrier, CHIPS)
    send(0)
    away.start()
    for load in loads:
        load.start()
    pack(1)
    send(1)
    receive(0)
    for load in loads:
        load.wait()

    def first(i, carry):
        block = rows[0, pl.ds(i * CHIPS, CHIPS)].reshape(group, width)
        here = pl.ds(pl.multiple_of(i * group, group), group)
        for j in range(units // 256):
            some = slice(j * 256, j * 256 + 256)
            pre_gate = dot(block, gate[:, some], (1, 0))
            pre_up = dot(block, up[:, some], (1, 0))
            pre[0, here, some] = pre_gate
            pre[1, here, some] = pre_up
            hidden[here, some] = (pre_gate * jax.nn.sigmoid(pre_gate) * pre_up).astype(jnp.bfloat16)
        return carry

    lax.fori_loop(0, 2, first, 0)

    def second(j, carry):
        columns = pl.ds(pl.multiple_of(j * step, step), step)
        for i in range(2):
            part = dot(hidden[i * group : i * group + group, :], down[:, columns], (1, 0))
            out[i * CHIPS : i * CHIPS + CHIPS, :, columns] = part.astype(jnp.bfloat16).reshape(
                CHIPS, CAP, step
            )
        return carry

    lax.fori_loop(0, 7, second, 0)
    store = pltpu.make_async_copy(out, out_part, out_sem.at[0])
    store.start()

    receive(1)

    def third(i, carry):
        block = rows[1, pl.ds(i * CHIPS, CHIPS)].reshape(group, width)
        here = pl.ds(pl.multiple_of(i * group, group), group)
        for j in range(units // 256):
            some = slice(j * 256, j * 256 + 256)
            hidden_grad = dot(block, down[some, :], (1, 1))
            pre_gate = pre[0, here, some]
            sigma = jax.nn.sigmoid(pre_gate)
            slope = sigma * (1.0 + pre_gate * (1.0 - sigma))
            gate_grad[here, some] = (hidden_grad * pre[1, here, some] * slope).astype(jnp.bfloat16)
            up_grad[here, some] = (hidden_grad * (pre_gate * sigma)).astype(jnp.bfloat16)
        return carry

    lax.fori_loop(0, 2, third, 0)

    store.wait()
    away.wait()
    for a in range(2):
        keeps[a].wait()
        for k in range(CHIPS):
            near(a, k).wait_send()
            if k:
                far(a, k).wait_send()


def forward(tokens, grads, packing, away_weight, w_gate, w_up, w_down):
    width = tokens.shape[1]
    units = w_gate.shape[1]
    anywhere = pl.BlockSpec(memory_space=pl.ANY)
    vmem = pl.BlockSpec(memory_space=pltpu.VMEM)
    dma = pltpu.SemaphoreType.DMA
    kind = tokens.dtype
    blocks = (2 * CHIPS, CAP, width)
    count = 2 * CHIPS * CAP
    many = jax.ShapeDtypeStruct(blocks, kind)
    inner = jax.ShapeDtypeStruct((count, units), kind)
    return pl.pallas_call(
        forward_kernel,
        name="forward",
        out_shape=(
            many,
            many,
            jax.ShapeDtypeStruct(away_weight.shape, kind),
            inner,
            inner,
            inner,
            many,
        ),
        in_specs=[vmem] * 3 + [anywhere] * 4,
        out_specs=(anywhere, anywhere, anywhere, vmem, vmem, vmem, anywhere),
        scratch_shapes=[
            pltpu.VMEM((2, CHIPS, CAP, width), kind),
            pltpu.VMEM((2, *blocks), kind),
            pltpu.VMEM(w_gate.shape, kind),
            pltpu.VMEM(w_up.shape, kind),
            pltpu.VMEM(w_down.shape, kind),
            pltpu.VMEM((2, count, units), jnp.float32),
            pltpu.VMEM(blocks, kind),
        ]
        + [dma((2, CHIPS))] * 4
        + [dma((3,)), dma((2,)), dma((1,)), dma((2,))],
        compiler_params=pltpu.CompilerParams(
            collective_id=1, has_side_effects=True, vmem_limit_bytes=58 << 20
        ),
    )(tokens, grads, packing, away_weight, w_gate, w_up, w_down)


def return_kernel(
    out_part,
    input_part,
    own_weight,
    relay_weight,
    out_acts,
    grad_acts,
    halves,
    mine,
    sums,
    landing,
    partial,
    remote,
    near_send,
    near_recv,
    mine_sem,
    send_sem,
    recv_sem,
    across_send,
    across_recv,
):
    pipe, own, y, z, core = place()
    arrays = (out_part, input_part)
    results = (out_acts, grad_acts)
    sibling = own + 1 - 2 * core
    opposite = (own + CHIPS) % (2 * CHIPS)

    barrier = pltpu.get_barrier_semaphore()
    for peer in [(y * 4 + (z + dz) % 4) * 2 + core for dz in range(1, 4)] + [sibling, opposite]:
        pl.semaphore_signal(barrier, inc=1, device_id=(pipe, peer), device_id_type=MESH)
    pl.semaphore_wait(barrier, 5)

    def near(a, k):
        there = chip_at(y, z, k, 1) * 2 + 1 - core
        return pltpu.make_async_remote_copy(
            src_ref=arrays[a].at[there],
            dst_ref=halves.at[a, k],
            send_sem=near_send.at[a, k],
            recv_sem=near_recv.at[a, k],
            device_id=(pipe, sibling),
            device_id_type=MESH,
        )

    def load(a, k):
        here = chip_at(y, z, k, 1) * 2 + core
        return pltpu.make_async_copy(arrays[a].at[here], mine.at[a, k], mine_sem.at[a, k])

    def along(a, k):
        return pltpu.make_async_remote_copy(
            src_ref=sums.at[a, k],
            dst_ref=landing.at[a, k // 4, z],
            send_sem=send_sem.at[a, k],
            recv_sem=recv_sem.at[a, k],
            device_id=(pipe, (y * 4 + (z + k % 4) % 4) * 2 + core),
            device_id_type=MESH,
        )

    def across(a):
        return pltpu.make_async_remote_copy(
            src_ref=partial.at[a],
            dst_ref=remote.at[a],
            send_sem=across_send.at[a],
            recv_sem=across_recv.at[a],
            device_id=(pipe, opposite),
            device_id_type=MESH,
        )

    width = out_acts.shape[1]
    step = width // 7

    def combine(a, dy, weight, put):
        for k in range(4 * dy + 1, 4 * dy + 4):
            along(a, k).wait_recv()

        def tile(j, carry):
            columns = pl.ds(pl.multiple_of(j * step, step), step)
            rows = landing[a, dy, :, :, columns].reshape(4 * CAP, step)
            if a == 0:
                total = jnp.dot(weight[0], rows, preferred_element_type=jnp.float32)
                total += jnp.dot(weight[1], rows, preferred_element_type=jnp.float32)
            else:
                total = jnp.dot(weight[2], rows, preferred_element_type=jnp.float32)
            put(columns, total)
            return carry

        lax.fori_loop(0, width // step, tile, 0)

    order = [(a, 4 * dy + dz) for dy in (1, 0) for a in range(2) for dz in (2, 1, 3, 0)]
    for a, k in order:
        near(a, k).start()
        load(a, k).start()
    for a, k in order:
        load(a, k).wait()
        near(a, k).wait_recv()
        total = halves[a, k].astype(jnp.float32) + mine[a, k].astype(jnp.float32)
        if k % 4:
            sums[a, k] = total.astype(jnp.bfloat16)
            along(a, k).start()
        else:
            landing[a, k // 4, z] = total.astype(jnp.bfloat16)
    for a in range(2):

        def send_on(columns, total, a=a):
            partial[a, :, columns] = total.astype(jnp.bfloat16)

        combine(a, 1, relay_weight, send_on)
        across(a).start()
    for a in range(2):
        across(a).wait_recv()

        def finish(columns, total, a=a):
            total = total + remote[a, :, columns].astype(jnp.float32)
            results[a][:, columns] = total.astype(jnp.bfloat16)

        combine(a, 0, own_weight, finish)
    for a in range(2):
        across(a).wait_send()
        for k in range(CHIPS):
            near(a, k).wait_send()
            if k % 4:
                along(a, k).wait_send()


def give_back(out_part, input_part, own_weight, relay_weight):
    width = out_part.shape[-1]
    count = own_weight.shape[1]
    anywhere = pl.BlockSpec(memory_space=pl.ANY)
    vmem = pl.BlockSpec(memory_space=pltpu.VMEM)
    dma = pltpu.SemaphoreType.DMA
    shape = jax.ShapeDtypeStruct((count, width), out_part.dtype)
    block = pltpu.VMEM((2, CHIPS, CAP, width), out_part.dtype)
    sent = pltpu.VMEM((2, count, width), out_part.dtype)
    return pl.pallas_call(
        return_kernel,
        name="give_back",
        out_shape=(shape, shape),
        in_specs=[anywhere, anywhere, vmem, vmem],
        out_specs=(vmem, vmem),
        scratch_shapes=[block] * 3
        + [pltpu.VMEM((2, 2, 4, CAP, width), out_part.dtype), sent, sent]
        + [dma((2, CHIPS))] * 5
        + [dma((2,))] * 2,
        compiler_params=pltpu.CompilerParams(
            collective_id=2, has_side_effects=True, vmem_limit_bytes=48 << 20
        ),
    )(out_part, input_part, own_weight, relay_weight)


def on_device(acts, grad_out, expert_ids, route_weights, w_gate, w_up, w_down):
    tokens, grads, ids, gain = acts[0], grad_out[0], expert_ids[0], route_weights[0]
    gate_weight, up_weight, down_weight = w_gate[0], w_up[0], w_down[0]
    count, top = ids.shape
    width = tokens.shape[1]
    units = gate_weight.shape[1]

    flat = ids.reshape(-1)
    member = (flat[:, None] == jnp.arange(CHIPS, dtype=jnp.int32)[None, :]).astype(jnp.bfloat16)
    before = jnp.tril(jnp.ones((count * top, count * top), jnp.bfloat16), -1)
    rank = jnp.sum(dot(before, member, (1, 0)) * member.astype(jnp.float32), axis=1)
    slot = (flat * CAP + rank.astype(jnp.int32)).reshape(count, top)
    hits = (slot[:, :, None] == jnp.arange(CHIPS * CAP, dtype=jnp.int32)).astype(jnp.float32)
    placing = jnp.sum(hits, axis=1).astype(jnp.bfloat16)
    high, low = split_gain(jnp.sum(hits * gain[:, :, None], axis=1))

    weights = jnp.stack([high, low, placing])
    side = lax.axis_index("expert") // CHIPS
    own_weight = lax.dynamic_slice_in_dim(weights, side * (4 * CAP), 4 * CAP, 2)
    away_weight = lax.dynamic_slice_in_dim(weights, (1 - side) * (4 * CAP), 4 * CAP, 2)
    packing = weights.swapaxes(1, 2)
    rows_in, rows_grad, relay_weight, hidden, gate_grad, up_grad, out_part = forward(
        tokens, grads, packing, away_weight, gate_weight, up_weight, down_weight
    )
    rows_in = rows_in.reshape(2 * CHIPS * CAP, width)
    rows_grad = rows_grad.reshape(2 * CHIPS * CAP, width)

    pipe = lax.axis_index("pipe")
    ranks = lax.axis_size("pipe")
    half = units // 2
    kept = (pipe >= ranks // 2).astype(jnp.int32) * half
    mirror = [(p, ranks - 1 - p) for p in range(ranks)]

    def cut(array, start):
        return lax.dynamic_slice_in_dim(array, start, half, 1)

    gave = [
        lax.ppermute(part.astype(jnp.bfloat16), "pipe", mirror)
        for part in (
            dot(rows_in, cut(gate_grad, half - kept), (0, 0)),
            dot(rows_in, cut(up_grad, half - kept), (0, 0)),
            dot(cut(hidden, half - kept), rows_grad, (0, 0)),
        )
    ]

    input_part = (dot(gate_grad, gate_weight, (1, 1)) + dot(up_grad, up_weight, (1, 1))).astype(
        jnp.bfloat16
    )
    kept_parts = [
        part.astype(jnp.bfloat16)
        for part in (
            dot(rows_in, cut(gate_grad, kept), (0, 0)),
            dot(rows_in, cut(up_grad, kept), (0, 0)),
            dot(cut(hidden, kept), rows_grad, (0, 0)),
        )
    ]
    kept_parts, out_part, input_part = lax.optimization_barrier((kept_parts, out_part, input_part))
    out_acts, grad_acts = give_back(
        out_part,
        input_part.reshape(2 * CHIPS, CAP, width),
        own_weight,
        relay_weight,
    )
    sums = [
        (part.astype(jnp.float32) + other.astype(jnp.float32)).astype(jnp.bfloat16)[None]
        for part, other in zip(kept_parts, gave)
    ]
    return (out_acts[None], grad_acts[None], *sums)


def solution(mesh):
    rows = P("pipe", "expert", None)
    columns = P("pipe", None, "expert")
    return jax.shard_map(
        on_device,
        mesh=mesh,
        in_specs=(rows, rows, rows, rows, columns, columns, rows),
        out_specs=(rows, rows, columns, columns, rows),
        check_vma=False,
    )
```

```python
import functools

import jax
import jax.numpy as jnp
from jax import lax
from jax.experimental import pallas as pl
from jax.experimental.pallas import tpu as pltpu
from jax.sharding import PartitionSpec as P

MESH = pl.DeviceIdType.MESH
CHIPS = 8
CAP = 48


def place():
    pipe = lax.axis_index("pipe")
    own = lax.axis_index("expert")
    return pipe, own, own // 8, (own // 2) % 4, own % 2


def chip_at(y, z, k, sign):
    return ((y + k // 4) % 2) * 4 + (z + 4 + sign * (k % 4)) % 4


def split_gain(gain):
    high = lax.reduce_precision(gain, exponent_bits=8, mantissa_bits=7)
    low = lax.reduce_precision(gain - high, exponent_bits=8, mantissa_bits=7)
    return high.astype(jnp.bfloat16), low.astype(jnp.bfloat16)


def dot(a, b, contract):
    dims = ((contract[:1], contract[1:]), ((), ()))
    return lax.dot_general(a, b, dims, preferred_element_type=jnp.float32)


def layer_kernel(
    tokens,
    grads,
    own_weight,
    away_weight,
    w_gate,
    w_up,
    w_down,
    out_acts,
    grad_acts,
    grad_gate,
    grad_up,
    grad_down,
    mirror_in,
    relay_weight,
    mine,
    raw,
    other,
    slots,
    rows,
    gate,
    up,
    down,
    pre,
    hidden,
    gate_grad,
    up_grad,
    factors,
    mirror_factors,
    out,
    halves,
    landing,
    other_down,
    stage,
    far_send,
    far_recv,
    near_send,
    near_recv,
    half_send,
    half_recv,
    along_send,
    along_recv,
    mirror_send,
    mirror_recv,
    pass_send,
    pass_recv,
    raw_send,
    raw_recv,
    across_send,
    across_recv,
    swap_send,
    swap_recv,
    away_sem,
    load_sem,
    stage_sem,
    result_sem,
):
    pipe, own, y, z, core = place()
    sibling = own + 1 - 2 * core
    opposite = (own + CHIPS) % (2 * CHIPS)
    ranks = lax.axis_size("pipe")
    mirrored = ranks - 1 - pipe
    kept = pipe // (ranks // 2)
    width = tokens.shape[1]
    units = w_gate.shape[1]
    step = width // 7
    group = CHIPS * CAP
    half = units // 2
    peers = [(y * 4 + (z + dz) % 4) * 2 + core for dz in range(4)]

    barrier = pltpu.get_barrier_semaphore()
    for peer in peers[1:] + [sibling, opposite]:
        pl.semaphore_signal(barrier, inc=1, device_id=(pipe, peer), device_id_type=MESH)
    pl.semaphore_signal(barrier, inc=1, device_id=(mirrored, own), device_id_type=MESH)

    loads = [
        pltpu.make_async_copy(source, target, load_sem.at[i])
        for i, (source, target) in enumerate(
            (
                (tokens, mine.at[0]),
                (grads, mine.at[1]),
                (w_gate, gate),
                (w_up, up),
                (w_down, down),
                (mirror_in, rows.at[1]),
            )
        )
    ]
    for load in loads[:5]:
        load.start()

    def origin(k):
        return chip_at(y, z, k, -1) * 2 + core

    def remote(source, target, sent, got, device):
        return pltpu.make_async_remote_copy(
            src_ref=source,
            dst_ref=target,
            send_sem=sent,
            recv_sem=got,
            device_id=device,
            device_id_type=MESH,
        )

    away = remote(away_weight, relay_weight, away_sem.at[0], away_sem.at[1], (pipe, opposite))

    def cross_raw(a):
        return remote(mine.at[a], raw.at[a], raw_send.at[a], raw_recv.at[a], (pipe, opposite))

    def far(a, k):
        dz = k % 4
        source = slots.at[a * 8 + (k // 4) * 4 + (z + dz) % 4]
        target = rows.at[a, (((y + k // 4) % 2) * 4 + z) * 2 + core]
        return remote(source, target, far_send.at[a, k], far_recv.at[a, k], (pipe, peers[dz]))

    def near(a, k):
        target = rows.at[a, origin(k)]
        source = target if k % 4 else slots.at[a * 8 + (k // 4) * 4 + z]
        return remote(source, target, near_send.at[a, k], near_recv.at[a, k], (pipe, sibling))

    def to_mirror(k):
        source = rows.at[0, origin(k)]
        target = mirror_in.at[origin(k)]
        return remote(source, target, mirror_send.at[k], mirror_recv.at[k], (mirrored, own))

    def pass_on(k):
        block = mirror_in.at[origin(k)]
        return remote(block, block, pass_send.at[k], pass_recv.at[k], (pipe, sibling))

    def swap(i):
        source = down.at[pl.ds(0, half)] if i == 2 else factors.at[i, 1 - kept]
        target = other_down if i == 2 else mirror_factors.at[i]
        return remote(source, target, swap_send.at[i], swap_recv.at[i], (mirrored, own))

    parts = (out, slots)

    def give_half(a, k):
        source = parts[a].at[chip_at(y, z, k, 1) * 2 + 1 - core]
        target = halves.at[a, k]
        return remote(source, target, half_send.at[a, k], half_recv.at[a, k], (pipe, sibling))

    def along(a, k):
        source = parts[a].at[chip_at(y, z, k, 1) * 2 + core]
        target = landing.at[a, k // 4, z]
        device = (pipe, peers[k % 4])
        return remote(source, target, along_send.at[a, k], along_recv.at[a, k], device)

    def across(a):
        return remote(
            mine.at[a], other.at[a], across_send.at[a], across_recv.at[a], (pipe, opposite)
        )

    results = [
        pltpu.make_async_copy(source, target, result_sem.at[i])
        for i, (source, target) in enumerate(
            (
                (raw.at[0], out_acts),
                (raw.at[1], grad_acts),
                (down.at[pl.ds(half, half)], grad_down),
            )
        )
    ]

    def tiles(body):
        def tile(j, carry):
            body(pl.ds(pl.multiple_of(j * step, step), step))
            return carry

        lax.fori_loop(0, 7, tile, 0)

    def pack(a, side):
        weight = relay_weight if side else own_weight
        source = raw if side else mine
        first = a * 8 + side * 4

        def tile(columns):
            part = source[a, :, columns]
            if a == 0:
                total = dot(weight[2], part, (0, 0))
            else:
                total = dot(weight[0], part, (0, 0)) + dot(weight[1], part, (0, 0))
            slots[first : first + 4, :, columns] = total.astype(jnp.bfloat16).reshape(4, CAP, step)

        tiles(tile)

    def send(a, side):
        for k in (2, 1, 3):
            far(a, 4 * side + k).start()
        near(a, 4 * side).start()
        rows[a, origin(4 * side)] = slots[a * 8 + side * 4 + z]

    def receive(a, side):
        for k in (1, 3, 2):
            far(a, 4 * side + k).wait_recv()
            near(a, 4 * side + k).start()

    def mirror(side):
        for k in range(4):
            to_mirror(4 * side + k).start()

    def settle(a):
        for k in range(CHIPS):
            near(a, k).wait_recv()

    def pass_side(side):
        for k in range(4):
            to_mirror(4 * side + k).wait_recv()
            pass_on(4 * side + k).start()

    order = [4 * dy + dz for dy in (1, 0) for dz in (2, 1, 3, 0)]

    def add_halves(a):
        for k in order:
            here = chip_at(y, z, k, 1) * 2 + core
            give_half(a, k).wait_recv()
            total = halves[a, k].astype(jnp.float32) + parts[a][here].astype(jnp.float32)
            if k % 4:
                parts[a][here] = total.astype(jnp.bfloat16)
                along(a, k).start()
            else:
                landing[a, k // 4, z] = total.astype(jnp.bfloat16)

    def combine(a, dy, weight, put):
        for k in range(4 * dy + 1, 4 * dy + 4):
            along(a, k).wait_recv()

        def tile(columns):
            block = landing[a, dy, :, :, columns].reshape(4 * CAP, step)
            if a == 0:
                total = dot(weight[0], block, (1, 0)) + dot(weight[1], block, (1, 0))
            else:
                total = dot(weight[2], block, (1, 0))
            put(columns, total)

        tiles(tile)

    loads[0].wait()
    pl.semaphore_wait(barrier, 6)
    away.start()
    cross_raw(0).start()
    pack(0, 0)
    send(0, 0)
    loads[1].wait()
    pack(1, 0)
    send(1, 0)
    cross_raw(0).wait_send()
    cross_raw(1).start()
    away.wait()
    cross_raw(0).wait_recv()
    pack(0, 1)
    send(0, 1)
    receive(0, 0)
    cross_raw(1).wait_recv()
    pack(1, 1)
    send(1, 1)
    mirror(0)
    receive(0, 1)
    mirror(1)
    settle(0)
    for load in loads[2:5]:
        load.wait()

    def units_of(i, carry):
        block = rows[0, pl.ds(i * CHIPS, CHIPS)].reshape(group, width)
        here = pl.ds(pl.multiple_of(i * group, group), group)
        for j in range(2):
            some = slice(j * half, j * half + half)
            pre_gate = dot(block, gate[:, some], (1, 0))
            pre_up = dot(block, up[:, some], (1, 0))
            pre[0, here, some] = pre_gate
            pre[1, here, some] = pre_up
            value = pre_gate * jax.nn.sigmoid(pre_gate) * pre_up
            hidden[here, some] = value.astype(jnp.bfloat16)
            factors[2, j, :, here] = value.T.astype(jnp.bfloat16)
        return carry

    lax.fori_loop(0, 2, units_of, 0)

    def out_tile(columns):
        for i in range(2):
            part = dot(hidden[i * group : i * group + group, :], down[:, columns], (1, 0))
            out[i * CHIPS : i * CHIPS + CHIPS, :, columns] = part.astype(jnp.bfloat16).reshape(
                CHIPS, CAP, step
            )

    tiles(out_tile)
    for k in order:
        give_half(0, k).start()
    receive(1, 0)
    receive(1, 1)
    settle(1)

    def grads_of(i, carry):
        block = rows[1, pl.ds(i * CHIPS, CHIPS)].reshape(group, width)
        here = pl.ds(pl.multiple_of(i * group, group), group)
        for j in range(2):
            some = slice(j * half, j * half + half)
            hidden_grad = dot(block, down[some, :], (1, 1))
            pre_gate = pre[0, here, some]
            sigma = jax.nn.sigmoid(pre_gate)
            slope = sigma * (1.0 + pre_gate * (1.0 - sigma))
            for_gate = hidden_grad * pre[1, here, some] * slope
            for_up = hidden_grad * (pre_gate * sigma)
            gate_grad[here, some] = for_gate.astype(jnp.bfloat16)
            up_grad[here, some] = for_up.astype(jnp.bfloat16)
            factors[0, j, :, here] = for_gate.T.astype(jnp.bfloat16)
            factors[1, j, :, here] = for_up.T.astype(jnp.bfloat16)
        return carry

    lax.fori_loop(0, 2, grads_of, 0)
    for i in range(2):
        swap(i).start()
    add_halves(0)

    for a in range(2):
        for k in range(CHIPS):
            near(a, k).wait_send()
            if k % 4:
                far(a, k).wait_send()

    def input_tile(columns):
        for i in range(2):
            here = slice(i * group, i * group + group)
            part = dot(gate_grad[here, :], gate[columns, :], (1, 1))
            part += dot(up_grad[here, :], up[columns, :], (1, 1))
            slots[i * CHIPS : i * CHIPS + CHIPS, :, columns] = part.astype(jnp.bfloat16).reshape(
                CHIPS, CAP, step
            )

    tiles(input_tile)
    for k in order:
        give_half(1, k).start()

    def down_tile(columns):
        block = rows[1, :, :, columns].reshape(2 * group, step)
        down[:half, columns] = dot(factors[2, 1 - kept], block, (1, 0)).astype(jnp.bfloat16)
        down[half:, columns] = dot(factors[2, kept], block, (1, 0)).astype(jnp.bfloat16)

    tiles(down_tile)
    swap(2).start()
    add_halves(1)
    pass_side(0)
    pass_side(1)

    for a in range(2):
        if a == 0:
            cross_raw(1).wait_send()

        def send_on(columns, total, a=a):
            mine[a, :, columns] = total.astype(jnp.bfloat16)

        combine(a, 1, relay_weight, send_on)
        across(a).start()

    for k in range(CHIPS):
        pass_on(k).wait_recv()
    loads[5].start()
    for i in range(2):
        swap(i).wait_recv()
    loads[5].wait()
    targets = (grad_gate, grad_up)

    def staged(j, i):
        columns = pl.ds(pl.multiple_of(j * step, step), step)
        slot = j % 2
        return pltpu.make_async_copy(
            stage.at[slot, i], targets[i].at[:, columns], stage_sem.at[slot, i]
        )

    def weight_tile(j, carry):
        columns = pl.ds(pl.multiple_of(j * step, step), step)
        mine_rows = rows[0, :, :, columns].reshape(2 * group, step)
        their_rows = rows[1, :, :, columns].reshape(2 * group, step)
        for i in range(2):

            @pl.when(j >= 2)
            def _(i=i):
                staged(j - 2, i).wait()

            total = dot(factors[i, kept], mine_rows, (1, 0))
            total += dot(mirror_factors[i], their_rows, (1, 0))
            stage[j % 2, i] = total.astype(jnp.bfloat16)
            staged(j, i).start()
        return carry

    lax.fori_loop(0, 7, weight_tile, 0)

    for a in range(2):
        across(a).wait_recv()

        def finish(columns, total, a=a):
            total = total + other[a, :, columns].astype(jnp.float32)
            raw[a, :, columns] = total.astype(jnp.bfloat16)

        combine(a, 0, own_weight, finish)
        results[a].start()
    swap(2).wait_recv()

    def down_sum(columns):
        total = down[half:, columns].astype(jnp.float32) + other_down[:, columns].astype(jnp.float32)
        down[half:, columns] = total.astype(jnp.bfloat16)

    tiles(down_sum)
    results[2].start()

    for j in (5, 6):
        for i in range(2):
            staged(j, i).wait()
    for result in results:
        result.wait()
    for i in range(3):
        swap(i).wait_send()
    for a in range(2):
        across(a).wait_send()
        for k in range(CHIPS):
            give_half(a, k).wait_send()
            if k % 4:
                along(a, k).wait_send()
    for k in range(CHIPS):
        to_mirror(k).wait_send()
        pass_on(k).wait_send()


def layer(tokens, grads, own_weight, away_weight, w_gate, w_up, w_down):
    count, width = tokens.shape
    units = w_gate.shape[1]
    half = units // 2
    anywhere = pl.BlockSpec(memory_space=pl.ANY)
    vmem = pl.BlockSpec(memory_space=pltpu.VMEM)
    dma = pltpu.SemaphoreType.DMA
    kind = tokens.dtype
    blocks = (2 * CHIPS, CAP, width)
    total = 2 * CHIPS * CAP
    ours = jax.ShapeDtypeStruct((count, width), kind)
    weight = jax.ShapeDtypeStruct((half, width), kind)
    return pl.pallas_call(
        layer_kernel,
        name="layer",
        out_shape=(ours, ours, weight, weight, weight, jax.ShapeDtypeStruct(blocks, kind)),
        in_specs=[anywhere] * 2 + [vmem] + [anywhere] * 4,
        out_specs=(anywhere,) * 6,
        scratch_shapes=[
            pltpu.VMEM(own_weight.shape, kind),
            pltpu.VMEM((2, count, width), kind),
            pltpu.VMEM((2, count, width), kind),
            pltpu.VMEM((2, count, width), kind),
            pltpu.VMEM(blocks, kind),
            pltpu.VMEM((2, *blocks), kind),
            pltpu.VMEM(w_gate.shape, kind),
            pltpu.VMEM(w_up.shape, kind),
            pltpu.VMEM(w_down.shape, kind),
            pltpu.VMEM((2, total, units), jnp.float32),
            pltpu.VMEM((total, units), kind),
            pltpu.VMEM((total, units), kind),
            pltpu.VMEM((total, units), kind),
            pltpu.VMEM((3, 2, half, total), kind),
            pltpu.VMEM((2, half, total), kind),
            pltpu.VMEM(blocks, kind),
            pltpu.VMEM((2, CHIPS, CAP, width), kind),
            pltpu.VMEM((2, 2, 4, CAP, width), kind),
            pltpu.VMEM((half, width), kind),
            pltpu.VMEM((2, 2, half, width // 7), kind),
        ]
        + [dma((2, CHIPS))] * 8
        + [dma((CHIPS,))] * 4
        + [dma((2,))] * 4
        + [dma((3,))] * 2
        + [dma((2,)), dma((6,)), dma((2, 2)), dma((3,))],
        compiler_params=pltpu.CompilerParams(
            collective_id=1, has_side_effects=True, vmem_limit_bytes=62 << 20
        ),
    )(tokens, grads, own_weight, away_weight, w_gate, w_up, w_down)[:5]


def on_device(acts, grad_out, expert_ids, route_weights, w_gate, w_up, w_down):
    tokens, grads, ids, gain = acts[0], grad_out[0], expert_ids[0], route_weights[0]
    gate_weight, up_weight, down_weight = w_gate[0], w_up[0], w_down[0]
    count, top = ids.shape
    width = tokens.shape[1]
    units = gate_weight.shape[1]

    flat = ids.reshape(-1)
    member = (flat[:, None] == jnp.arange(CHIPS, dtype=jnp.int32)[None, :]).astype(jnp.bfloat16)
    before = jnp.tril(jnp.ones((count * top, count * top), jnp.bfloat16), -1)
    rank = jnp.sum(dot(before, member, (1, 0)) * member.astype(jnp.float32), axis=1)
    slot = (flat * CAP + rank.astype(jnp.int32)).reshape(count, top)
    hits = (slot[:, :, None] == jnp.arange(CHIPS * CAP, dtype=jnp.int32)).astype(jnp.float32)
    placing = jnp.sum(hits, axis=1).astype(jnp.bfloat16)
    high, low = split_gain(jnp.sum(hits * gain[:, :, None], axis=1))

    weights = jnp.stack([high, low, placing])
    side = lax.axis_index("expert") // CHIPS
    own_weight = lax.dynamic_slice_in_dim(weights, side * (4 * CAP), 4 * CAP, 2)
    away_weight = lax.dynamic_slice_in_dim(weights, (1 - side) * (4 * CAP), 4 * CAP, 2)
    out_acts, grad_acts, grad_gate, grad_up, grad_down = layer(
        tokens, grads, own_weight, away_weight, gate_weight, up_weight, down_weight
    )
    return (out_acts[None], grad_acts[None], grad_gate.T[None], grad_up.T[None], grad_down[None])


def solution(mesh):
    rows = P("pipe", "expert", None)
    columns = P("pipe", None, "expert")
    return jax.shard_map(
        on_device,
        mesh=mesh,
        in_specs=(rows, rows, rows, rows, columns, columns, rows),
        out_specs=(rows, rows, columns, columns, rows),
        check_vma=False,
    )
```

```python
import functools

import jax
import jax.numpy as jnp
from jax import lax
from jax.experimental import pallas as pl
from jax.experimental.pallas import tpu as pltpu
from jax.sharding import PartitionSpec as P

MESH = pl.DeviceIdType.MESH
CHIPS = 8
CAP = 48


def place():
    pipe = lax.axis_index("pipe")
    own = lax.axis_index("expert")
    return pipe, own, own // 8, (own // 2) % 4, own % 2


def chip_at(y, z, k, sign):
    return ((y + k // 4) % 2) * 4 + (z + 4 + sign * (k % 4)) % 4


def split_gain(gain):
    high = lax.reduce_precision(gain, exponent_bits=8, mantissa_bits=7)
    low = lax.reduce_precision(gain - high, exponent_bits=8, mantissa_bits=7)
    return high.astype(jnp.bfloat16), low.astype(jnp.bfloat16)


def dot(a, b, contract):
    dims = ((contract[:1], contract[1:]), ((), ()))
    return lax.dot_general(a, b, dims, preferred_element_type=jnp.float32)


def layer_kernel(
    tokens,
    grads,
    own_weight,
    away_weight,
    w_gate,
    w_up,
    w_down,
    out_acts,
    grad_acts,
    grad_gate,
    grad_up,
    grad_down,
    mirror_in,
    other_down,
    relay_weight,
    mirror_weight,
    mine,
    raw,
    mirror_raw,
    other,
    slots,
    mirror_slots,
    rows,
    gate,
    up,
    down,
    pre,
    hidden,
    gate_grad,
    up_grad,
    factors,
    mirror_factors,
    out,
    halves,
    landing,
    stage,
    far_send,
    far_recv,
    near_send,
    near_recv,
    half_send,
    half_recv,
    along_send,
    along_recv,
    mirror_send,
    mirror_recv,
    pass_send,
    pass_recv,
    raw_send,
    raw_recv,
    across_send,
    across_recv,
    swap_send,
    swap_recv,
    away_send,
    away_recv,
    relay_send,
    relay_recv,
    load_sem,
    stage_sem,
    result_sem,
    free_sem,
):
    pipe, own, y, z, core = place()
    sibling = own + 1 - 2 * core
    opposite = (own + CHIPS) % (2 * CHIPS)
    ranks = lax.axis_size("pipe")
    mirrored = ranks - 1 - pipe
    kept = pipe // (ranks // 2)
    width = tokens.shape[1]
    units = w_gate.shape[1]
    step = width // 7
    group = CHIPS * CAP
    half = units // 2
    peers = [(y * 4 + (z + dz) % 4) * 2 + core for dz in range(4)]

    barrier = pltpu.get_barrier_semaphore()
    for peer in peers[1:] + [sibling, opposite]:
        pl.semaphore_signal(barrier, inc=1, device_id=(pipe, peer), device_id_type=MESH)
    for peer in (own, opposite):
        pl.semaphore_signal(barrier, inc=1, device_id=(mirrored, peer), device_id_type=MESH)

    loads = [
        pltpu.make_async_copy(source, target, load_sem.at[i])
        for i, (source, target) in enumerate(
            (
                (tokens, mine.at[0]),
                (grads, mine.at[1]),
                (w_gate, gate),
                (w_up, up),
                (w_down, down),
                (mirror_in, rows.at[1]),
                (other_down, down.at[pl.ds(0, half)]),
                (mirror_slots.at[z], mirror_in.at[own]),
                (mirror_slots.at[4 + z], mirror_in.at[opposite]),
            )
        )
    ]
    for load in loads[:5]:
        load.start()

    def origin(k):
        return chip_at(y, z, k, -1) * 2 + core

    def remote(source, target, sent, got, device):
        return pltpu.make_async_remote_copy(
            src_ref=source,
            dst_ref=target,
            send_sem=sent,
            recv_sem=got,
            device_id=device,
            device_id_type=MESH,
        )

    placings = [
        remote(source, target, away_send.at[i], away_recv.at[i], device)
        for i, (source, target, device) in enumerate(
            (
                (away_weight, relay_weight, (pipe, opposite)),
                (own_weight.at[2], mirror_weight.at[0], (mirrored, own)),
                (away_weight.at[2], mirror_weight.at[1], (mirrored, opposite)),
            )
        )
    ]
    swap_raw = remote(
        mine.at[0], mirror_raw.at[1], relay_send.at[1], relay_recv.at[1], (mirrored, opposite)
    )
    relay_raw = remote(
        mirror_raw.at[1], mirror_raw.at[0], relay_send.at[0], relay_recv.at[0], (pipe, opposite)
    )

    def cross_raw(a):
        return remote(mine.at[a], raw.at[a], raw_send.at[a], raw_recv.at[a], (pipe, opposite))

    def far(a, k):
        dz = k % 4
        source = slots.at[a * 8 + (k // 4) * 4 + (z + dz) % 4]
        target = rows.at[a, (((y + k // 4) % 2) * 4 + z) * 2 + core]
        return remote(source, target, far_send.at[a, k], far_recv.at[a, k], (pipe, peers[dz]))

    def near(a, k):
        target = rows.at[a, origin(k)]
        source = target if k % 4 else slots.at[a * 8 + (k // 4) * 4 + z]
        return remote(source, target, near_send.at[a, k], near_recv.at[a, k], (pipe, sibling))

    def mirror_far(k):
        dz = k % 4
        source = mirror_slots.at[(k // 4) * 4 + (z + dz) % 4]
        target = mirror_in.at[(((y + k // 4) % 2) * 4 + z) * 2 + core]
        return remote(source, target, mirror_send.at[k], mirror_recv.at[k], (pipe, peers[dz]))

    def mirror_near(k):
        target = mirror_in.at[origin(k)]
        source = target if k % 4 else mirror_slots.at[(k // 4) * 4 + z]
        return remote(source, target, pass_send.at[k], pass_recv.at[k], (pipe, sibling))

    def swap(i):
        source = down.at[pl.ds(0, half)] if i == 2 else factors.at[i, 1 - kept]
        target = other_down if i == 2 else mirror_factors.at[i]
        return remote(source, target, swap_send.at[i], swap_recv.at[i], (mirrored, own))

    parts = (out, slots)

    def give_half(a, k):
        source = parts[a].at[chip_at(y, z, k, 1) * 2 + 1 - core]
        target = halves.at[k]
        return remote(source, target, half_send.at[a, k], half_recv.at[a, k], (pipe, sibling))

    def along(a, k):
        source = parts[a].at[chip_at(y, z, k, 1) * 2 + core]
        target = landing.at[a, k // 4, z]
        device = (pipe, peers[k % 4])
        return remote(source, target, along_send.at[a, k], along_recv.at[a, k], device)

    def across(a):
        return remote(
            mine.at[a], other.at[a], across_send.at[a], across_recv.at[a], (pipe, opposite)
        )

    results = [
        pltpu.make_async_copy(source, target, result_sem.at[i])
        for i, (source, target) in enumerate(
            (
                (raw.at[0], out_acts),
                (raw.at[1], grad_acts),
                (down.at[pl.ds(half, half)], grad_down),
            )
        )
    ]

    def tiles(body):
        def tile(j, carry):
            body(pl.ds(pl.multiple_of(j * step, step), step))
            return carry

        lax.fori_loop(0, 7, tile, 0)

    def pack(a, side):
        weight = relay_weight if side else own_weight
        source = raw if side else mine
        first = a * 8 + side * 4

        def tile(columns):
            part = source[a, :, columns]
            if a == 0:
                total = dot(weight[2], part, (0, 0))
            else:
                total = dot(weight[0], part, (0, 0)) + dot(weight[1], part, (0, 0))
            slots[first : first + 4, :, columns] = total.astype(jnp.bfloat16).reshape(4, CAP, step)

        tiles(tile)

    def send(a, side):
        for k in (2, 1, 3):
            far(a, 4 * side + k).start()
        near(a, 4 * side).start()
        rows[a, origin(4 * side)] = slots[a * 8 + side * 4 + z]

    def receive(a, side):
        for k in (1, 3, 2):
            far(a, 4 * side + k).wait_recv()
            near(a, 4 * side + k).start()

    def mirror_pack(side):
        def tile(columns):
            total = dot(mirror_weight[side], mirror_raw[side, :, columns], (0, 0))
            mirror_slots[side * 4 : side * 4 + 4, :, columns] = total.astype(jnp.bfloat16).reshape(
                4, CAP, step
            )

        tiles(tile)

    def mirror_send_on(side):
        for k in (2, 1, 3):
            mirror_far(4 * side + k).start()
        mirror_near(4 * side).start()
        loads[7 + side].start()

    def settle(a):
        for k in range(CHIPS):
            near(a, k).wait_recv()

    def mirror_receive(side):
        for k in (1, 3, 2):
            mirror_far(4 * side + k).wait_recv()
            mirror_near(4 * side + k).start()

    order = [4 * dy + dz for dy in (1, 0) for dz in (2, 1, 3, 0)]

    def add_halves(a):
        for k in order:
            here = chip_at(y, z, k, 1) * 2 + core
            give_half(a, k).wait_recv()
            total = halves[k].astype(jnp.float32) + parts[a][here].astype(jnp.float32)
            if k % 4:
                parts[a][here] = total.astype(jnp.bfloat16)
                along(a, k).start()
            else:
                landing[a, k // 4, z] = total.astype(jnp.bfloat16)

    def combine(a, dy, weight, put):
        for k in range(4 * dy + 1, 4 * dy + 4):
            along(a, k).wait_recv()

        def tile(columns):
            block = landing[a, dy, :, :, columns].reshape(4 * CAP, step)
            if a == 0:
                total = dot(weight[0], block, (1, 0)) + dot(weight[1], block, (1, 0))
            else:
                total = dot(weight[2], block, (1, 0))
            put(columns, total)

        tiles(tile)

    loads[0].wait()
    pl.semaphore_wait(barrier, 7)
    for placing in placings:
        placing.start()
    cross_raw(0).start()
    swap_raw.start()
    pack(0, 0)
    send(0, 0)
    loads[1].wait()
    pack(1, 0)
    send(1, 0)
    cross_raw(0).wait_send()
    cross_raw(1).start()
    placings[0].wait_recv()
    cross_raw(0).wait_recv()
    pack(0, 1)
    send(0, 1)
    receive(0, 0)
    for placing in placings[1:]:
        placing.wait_recv()
    swap_raw.wait_recv()
    mirror_pack(1)
    cross_raw(1).wait_recv()
    relay_raw.start()
    pack(1, 1)
    send(1, 1)
    receive(0, 1)
    settle(0)
    for load in loads[2:5]:
        load.wait()

    def units_of(i, carry):
        block = rows[0, pl.ds(i * CHIPS, CHIPS)].reshape(group, width)
        here = pl.ds(pl.multiple_of(i * group, group), group)
        for j in range(2):
            some = slice(j * half, j * half + half)
            pre_gate = dot(block, gate[:, some], (1, 0))
            pre_up = dot(block, up[:, some], (1, 0))
            pre[0, here, some] = pre_gate
            pre[1, here, some] = pre_up
            value = pre_gate * jax.nn.sigmoid(pre_gate) * pre_up
            hidden[here, some] = value.astype(jnp.bfloat16)
            factors[2, j, :, here] = value.T.astype(jnp.bfloat16)
        return carry

    lax.fori_loop(0, 2, units_of, 0)

    def out_tile(columns):
        for i in range(2):
            part = dot(hidden[i * group : i * group + group, :], down[:, columns], (1, 0))
            out[i * CHIPS : i * CHIPS + CHIPS, :, columns] = part.astype(jnp.bfloat16).reshape(
                CHIPS, CAP, step
            )

    tiles(out_tile)
    for k in order:
        give_half(0, k).start()
    mirror_send_on(1)
    receive(1, 0)
    receive(1, 1)
    settle(1)

    def grads_of(i, carry):
        block = rows[1, pl.ds(i * CHIPS, CHIPS)].reshape(group, width)
        here = pl.ds(pl.multiple_of(i * group, group), group)
        for j in range(2):
            some = slice(j * half, j * half + half)
            hidden_grad = dot(block, down[some, :], (1, 1))
            pre_gate = pre[0, here, some]
            sigma = jax.nn.sigmoid(pre_gate)
            slope = sigma * (1.0 + pre_gate * (1.0 - sigma))
            for_gate = hidden_grad * pre[1, here, some] * slope
            for_up = hidden_grad * (pre_gate * sigma)
            gate_grad[here, some] = for_gate.astype(jnp.bfloat16)
            up_grad[here, some] = for_up.astype(jnp.bfloat16)
            factors[0, j, :, here] = for_gate.T.astype(jnp.bfloat16)
            factors[1, j, :, here] = for_up.T.astype(jnp.bfloat16)
        return carry

    lax.fori_loop(0, 2, grads_of, 0)
    for i in range(2):
        swap(i).start()
    add_halves(0)
    pl.semaphore_signal(free_sem, inc=1, device_id=(pipe, sibling), device_id_type=MESH)

    for a in range(2):
        for k in range(CHIPS):
            near(a, k).wait_send()
            if k % 4:
                far(a, k).wait_send()

    def input_tile(columns):
        for i in range(2):
            here = slice(i * group, i * group + group)
            part = dot(gate_grad[here, :], gate[columns, :], (1, 1))
            part += dot(up_grad[here, :], up[columns, :], (1, 1))
            slots[i * CHIPS : i * CHIPS + CHIPS, :, columns] = part.astype(jnp.bfloat16).reshape(
                CHIPS, CAP, step
            )

    tiles(input_tile)
    pl.semaphore_wait(free_sem, 1)
    for k in order:
        give_half(1, k).start()

    def down_tile(columns):
        block = rows[1, :, :, columns].reshape(2 * group, step)
        down[:half, columns] = dot(factors[2, 1 - kept], block, (1, 0)).astype(jnp.bfloat16)
        down[half:, columns] = dot(factors[2, kept], block, (1, 0)).astype(jnp.bfloat16)

    tiles(down_tile)
    swap(2).start()
    add_halves(1)
    relay_raw.wait_recv()
    mirror_pack(0)
    mirror_send_on(0)
    mirror_receive(1)

    for a in range(2):
        if a == 0:
            cross_raw(1).wait_send()
            swap_raw.wait_send()

        def send_on(columns, total, a=a):
            mine[a, :, columns] = total.astype(jnp.bfloat16)

        combine(a, 1, relay_weight, send_on)
        across(a).start()

    mirror_receive(0)
    for k in range(CHIPS):
        mirror_near(k).wait_recv()
    loads[7].wait()
    loads[8].wait()
    loads[5].start()
    for i in range(2):
        swap(i).wait_recv()
    loads[5].wait()
    targets = (grad_gate, grad_up)

    def staged(j, i):
        columns = pl.ds(pl.multiple_of(j * step, step), step)
        slot = j % 2
        return pltpu.make_async_copy(
            stage.at[slot, i], targets[i].at[columns, :], stage_sem.at[slot, i]
        )

    def weight_tile(j, carry):
        columns = pl.ds(pl.multiple_of(j * step, step), step)
        mine_rows = rows[0, :, :, columns].reshape(2 * group, step)
        their_rows = rows[1, :, :, columns].reshape(2 * group, step)
        for i in range(2):

            @pl.when(j >= 2)
            def _(i=i):
                staged(j - 2, i).wait()

            total = dot(factors[i, kept], mine_rows, (1, 0))
            total += dot(mirror_factors[i], their_rows, (1, 0))
            stage[j % 2, i] = total.T.astype(jnp.bfloat16)
            staged(j, i).start()
        return carry

    lax.fori_loop(0, 7, weight_tile, 0)

    def finish_rows(a):
        across(a).wait_recv()

        def finish(columns, total):
            total = total + other[a, :, columns].astype(jnp.float32)
            raw[a, :, columns] = total.astype(jnp.bfloat16)

        combine(a, 0, own_weight, finish)
        results[a].start()

    def down_sum(columns):
        total = down[half:, columns].astype(jnp.float32) + down[:half, columns].astype(jnp.float32)
        down[half:, columns] = total.astype(jnp.bfloat16)

    finish_rows(0)
    swap(2).wait()
    loads[6].start()
    loads[6].wait()
    tiles(down_sum)
    results[2].start()
    finish_rows(1)

    for j in (5, 6):
        for i in range(2):
            staged(j, i).wait()
    for result in results:
        result.wait()
    for i in range(2):
        swap(i).wait_send()
    for placing in placings:
        placing.wait_send()
    relay_raw.wait_send()
    for a in range(2):
        across(a).wait_send()
        for k in range(CHIPS):
            give_half(a, k).wait_send()
            if k % 4:
                along(a, k).wait_send()
    for k in range(CHIPS):
        mirror_near(k).wait_send()
        if k % 4:
            mirror_far(k).wait_send()


def layer(tokens, grads, own_weight, away_weight, w_gate, w_up, w_down):
    count, width = tokens.shape
    units = w_gate.shape[1]
    half = units // 2
    anywhere = pl.BlockSpec(memory_space=pl.ANY)
    vmem = pl.BlockSpec(memory_space=pltpu.VMEM)
    dma = pltpu.SemaphoreType.DMA
    kind = tokens.dtype
    blocks = (2 * CHIPS, CAP, width)
    total = 2 * CHIPS * CAP
    ours = jax.ShapeDtypeStruct((count, width), kind)
    weight = jax.ShapeDtypeStruct((width, half), kind)
    down = jax.ShapeDtypeStruct((half, width), kind)
    return pl.pallas_call(
        layer_kernel,
        name="layer",
        out_shape=(ours, ours, weight, weight, down, jax.ShapeDtypeStruct(blocks, kind), down),
        in_specs=[anywhere] * 2 + [vmem] + [anywhere] * 4,
        out_specs=(anywhere,) * 7,
        scratch_shapes=[
            pltpu.VMEM(own_weight.shape, kind),
            pltpu.VMEM((2, *own_weight.shape[1:]), kind),
            pltpu.VMEM((2, count, width), kind),
            pltpu.VMEM((2, count, width), kind),
            pltpu.VMEM((2, count, width), kind),
            pltpu.VMEM((2, count, width), kind),
            pltpu.VMEM(blocks, kind),
            pltpu.VMEM((CHIPS, CAP, width), kind),
            pltpu.VMEM((2, *blocks), kind),
            pltpu.VMEM(w_gate.shape, kind),
            pltpu.VMEM(w_up.shape, kind),
            pltpu.VMEM(w_down.shape, kind),
            pltpu.VMEM((2, total, units), jnp.float32),
            pltpu.VMEM((total, units), kind),
            pltpu.VMEM((total, units), kind),
            pltpu.VMEM((total, units), kind),
            pltpu.VMEM((3, 2, half, total), kind),
            pltpu.VMEM((2, half, total), kind),
            pltpu.VMEM(blocks, kind),
            pltpu.VMEM((CHIPS, CAP, width), kind),
            pltpu.VMEM((2, 2, 4, CAP, width), kind),
            pltpu.VMEM((2, 2, width // 7, half), kind),
        ]
        + [dma((2, CHIPS))] * 8
        + [dma((CHIPS,))] * 4
        + [dma((2,))] * 4
        + [dma((3,))] * 4
        + [dma((2,))] * 2
        + [dma((9,)), dma((2, 2)), dma((3,)), pltpu.SemaphoreType.REGULAR],
        compiler_params=pltpu.CompilerParams(
            collective_id=1, has_side_effects=True, vmem_limit_bytes=62 << 20
        ),
    )(tokens, grads, own_weight, away_weight, w_gate, w_up, w_down)[:5]


def on_device(acts, grad_out, expert_ids, route_weights, w_gate, w_up, w_down):
    tokens, grads, ids, gain = acts[0], grad_out[0], expert_ids[0], route_weights[0]
    gate_weight, up_weight, down_weight = w_gate[0], w_up[0], w_down[0]
    count, top = ids.shape
    width = tokens.shape[1]
    units = gate_weight.shape[1]

    flat = ids.reshape(-1)
    member = (flat[:, None] == jnp.arange(CHIPS, dtype=jnp.int32)[None, :]).astype(jnp.bfloat16)
    before = jnp.tril(jnp.ones((count * top, count * top), jnp.bfloat16), -1)
    rank = jnp.sum(dot(before, member, (1, 0)) * member.astype(jnp.float32), axis=1)
    slot = (flat * CAP + rank.astype(jnp.int32)).reshape(count, top)
    hits = (slot[:, :, None] == jnp.arange(CHIPS * CAP, dtype=jnp.int32)).astype(jnp.float32)
    placing = jnp.sum(hits, axis=1).astype(jnp.bfloat16)
    high, low = split_gain(jnp.sum(hits * gain[:, :, None], axis=1))

    weights = jnp.stack([high, low, placing])
    side = lax.axis_index("expert") // CHIPS
    own_weight = lax.dynamic_slice_in_dim(weights, side * (4 * CAP), 4 * CAP, 2)
    away_weight = lax.dynamic_slice_in_dim(weights, (1 - side) * (4 * CAP), 4 * CAP, 2)
    out_acts, grad_acts, grad_gate, grad_up, grad_down = layer(
        tokens, grads, own_weight, away_weight, gate_weight, up_weight, down_weight
    )
    return (out_acts[None], grad_acts[None], grad_gate[None], grad_up[None], grad_down[None])


def solution(mesh):
    rows = P("pipe", "expert", None)
    columns = P("pipe", None, "expert")
    return jax.shard_map(
        on_device,
        mesh=mesh,
        in_specs=(rows, rows, rows, rows, columns, columns, rows),
        out_specs=(rows, rows, columns, columns, rows),
        check_vma=False,
    )
```

```python
import functools

import jax
import jax.numpy as jnp
from jax import lax
from jax.experimental import pallas as pl
from jax.experimental.pallas import tpu as pltpu
from jax.sharding import PartitionSpec as P

MESH = pl.DeviceIdType.MESH
CHIPS = 8
CAP = 48


def place():
    pipe = lax.axis_index("pipe")
    own = lax.axis_index("expert")
    return pipe, own, own // 8, (own // 2) % 4, own % 2


def chip_at(y, z, k, sign):
    return ((y + k // 4) % 2) * 4 + (z + 4 + sign * (k % 4)) % 4


def dot(a, b, contract):
    dims = ((contract[:1], contract[1:]), ((), ()))
    return lax.dot_general(a, b, dims, preferred_element_type=jnp.float32)


def layer_kernel(
    tokens,
    grads,
    ids,
    gain,
    w_gate,
    w_up,
    w_down,
    out_terms,
    input_terms,
    out_other,
    input_other,
    grad_gate,
    grad_up,
    own_down,
    other_down,
    mirror_in,
    own_weight,
    away_weight,
    relay_weight,
    mirror_weight,
    mine,
    raw,
    mirror_raw,
    slots,
    mirror_slots,
    rows,
    gate,
    up,
    down,
    pre,
    hidden,
    gate_grad,
    up_grad,
    factors,
    mirror_factors,
    out,
    halves,
    landing,
    away_half,
    stage,
    far_send,
    far_recv,
    near_send,
    near_recv,
    half_send,
    half_recv,
    along_send,
    along_recv,
    mirror_send,
    mirror_recv,
    pass_send,
    pass_recv,
    raw_send,
    raw_recv,
    across_send,
    across_recv,
    swap_send,
    swap_recv,
    down_sem,
    away_send,
    away_recv,
    relay_send,
    relay_recv,
    load_sem,
    stage_sem,
    result_sem,
    free_sem,
):
    pipe, own, y, z, core = place()
    sibling = own + 1 - 2 * core
    opposite = (own + CHIPS) % (2 * CHIPS)
    ranks = lax.axis_size("pipe")
    mirrored = ranks - 1 - pipe
    kept = pipe // (ranks // 2)
    width = tokens.shape[1]
    units = w_gate.shape[1]
    step = width // 7
    group = CHIPS * CAP
    half = units // 2
    peers = [(y * 4 + (z + dz) % 4) * 2 + core for dz in range(4)]

    barrier = pltpu.get_barrier_semaphore()
    for peer in peers[1:] + [sibling, opposite]:
        pl.semaphore_signal(barrier, inc=1, device_id=(pipe, peer), device_id_type=MESH)
    for peer in (own, opposite):
        pl.semaphore_signal(barrier, inc=1, device_id=(mirrored, peer), device_id_type=MESH)

    loads = [
        pltpu.make_async_copy(source, target, load_sem.at[i])
        for i, (source, target) in enumerate(
            (
                (tokens, mine.at[0]),
                (grads, mine.at[1]),
                (w_gate, gate),
                (w_up, up),
                (w_down, down),
                (mirror_in, rows.at[1]),
                (mirror_slots.at[z], mirror_in.at[own]),
                (mirror_slots.at[4 + z], mirror_in.at[opposite]),
            )
        )
    ]
    for load in loads[:5]:
        load.start()

    def origin(k):
        return chip_at(y, z, k, -1) * 2 + core

    def remote(source, target, sent, got, device):
        return pltpu.make_async_remote_copy(
            src_ref=source,
            dst_ref=target,
            send_sem=sent,
            recv_sem=got,
            device_id=device,
            device_id_type=MESH,
        )

    placings = [
        remote(source, target, away_send.at[i], away_recv.at[i], device)
        for i, (source, target, device) in enumerate(
            (
                (away_weight, relay_weight, (pipe, opposite)),
                (own_weight.at[2], mirror_weight.at[0], (mirrored, own)),
                (away_weight.at[2], mirror_weight.at[1], (mirrored, opposite)),
            )
        )
    ]
    swap_raw = remote(
        mine.at[0], mirror_raw.at[1], relay_send.at[1], relay_recv.at[1], (mirrored, opposite)
    )
    relay_raw = remote(
        mirror_raw.at[1], mirror_raw.at[0], relay_send.at[0], relay_recv.at[0], (pipe, opposite)
    )

    def cross_raw(a):
        return remote(mine.at[a], raw.at[a], raw_send.at[a], raw_recv.at[a], (pipe, opposite))

    def far(a, k):
        dz = k % 4
        source = slots.at[a * 8 + (k // 4) * 4 + (z + dz) % 4]
        target = rows.at[a, (((y + k // 4) % 2) * 4 + z) * 2 + core]
        return remote(source, target, far_send.at[a, k], far_recv.at[a, k], (pipe, peers[dz]))

    def near(a, k):
        target = rows.at[a, origin(k)]
        source = target if k % 4 else slots.at[a * 8 + (k // 4) * 4 + z]
        return remote(source, target, near_send.at[a, k], near_recv.at[a, k], (pipe, sibling))

    def mirror_far(k):
        dz = k % 4
        source = mirror_slots.at[(k // 4) * 4 + (z + dz) % 4]
        target = mirror_in.at[(((y + k // 4) % 2) * 4 + z) * 2 + core]
        return remote(source, target, mirror_send.at[k], mirror_recv.at[k], (pipe, peers[dz]))

    def mirror_near(k):
        target = mirror_in.at[origin(k)]
        source = target if k % 4 else mirror_slots.at[(k // 4) * 4 + z]
        return remote(source, target, pass_send.at[k], pass_recv.at[k], (pipe, sibling))

    def swap(i, side):
        if i == 2:
            source, target = away_half, other_down
            return remote(source, target, down_sem.at[0], down_sem.at[1], (mirrored, own))
        some = pl.ds(pl.multiple_of(side * group, group), group)
        source = factors.at[i, 1 - kept, :, some]
        target = mirror_factors.at[i, :, some]
        return remote(source, target, swap_send.at[i, side], swap_recv.at[i, side], (mirrored, own))

    parts = (out, slots)

    def give_half(a, k):
        source = parts[a].at[chip_at(y, z, k, 1) * 2 + 1 - core]
        target = halves.at[k]
        return remote(source, target, half_send.at[a, k], half_recv.at[a, k], (pipe, sibling))

    def along(a, k):
        source = parts[a].at[chip_at(y, z, k, 1) * 2 + core]
        target = landing.at[a, k // 4, z]
        device = (pipe, peers[k % 4])
        return remote(source, target, along_send.at[a, k], along_recv.at[a, k], device)

    def across(a):
        target = (out_other, input_other)[a]
        return remote(mine.at[a], target, across_send.at[a], across_recv.at[a], (pipe, opposite))

    results = [
        pltpu.make_async_copy(source, target, result_sem.at[i])
        for i, (source, target) in enumerate(
            (
                (raw.at[0], out_terms),
                (raw.at[1], input_terms),
                (down.at[pl.ds(half, half)], own_down),
            )
        )
    ]

    def tiles(body):
        def tile(j, carry):
            body(pl.ds(pl.multiple_of(j * step, step), step))
            return carry

        lax.fori_loop(0, 7, tile, 0)

    def pack(a, side):
        weight = relay_weight if side else own_weight
        source = raw if side else mine
        first = a * 8 + side * 4

        def tile(columns):
            part = source[a, :, columns]
            if a == 0:
                total = dot(weight[2], part, (1, 0))
            else:
                total = dot(weight[0], part, (1, 0)) + dot(weight[1], part, (1, 0))
            slots[first : first + 4, :, columns] = total.astype(jnp.bfloat16).reshape(4, CAP, step)

        tiles(tile)

    def send(a, side):
        for k in (2, 1, 3):
            far(a, 4 * side + k).start()
        near(a, 4 * side).start()
        rows[a, origin(4 * side)] = slots[a * 8 + side * 4 + z]

    def receive(a, side):
        for k in (1, 3, 2):
            far(a, 4 * side + k).wait_recv()
            near(a, 4 * side + k).start()

    def mirror_pack(side):
        def tile(columns):
            total = dot(mirror_weight[side], mirror_raw[side, :, columns], (1, 0))
            mirror_slots[side * 4 : side * 4 + 4, :, columns] = total.astype(jnp.bfloat16).reshape(
                4, CAP, step
            )

        tiles(tile)

    def mirror_send_on(side):
        for k in (2, 1, 3):
            mirror_far(4 * side + k).start()
        mirror_near(4 * side).start()
        loads[6 + side].start()

    def settle(a, ks):
        for k in ks:
            near(a, k).wait_recv()

    def mirror_receive(side):
        for k in (1, 3, 2):
            mirror_far(4 * side + k).wait_recv()
            mirror_near(4 * side + k).start()

    def give_halves(a):
        for side in (1, 0):
            for dz in (2, 1, 3, 0):
                give_half(a, 4 * side + dz).start()

    def add_halves(a, side):
        for dz in (2, 1, 3, 0):
            k = 4 * side + dz
            here = chip_at(y, z, k, 1) * 2 + core
            give_half(a, k).wait_recv()
            total = halves[k].astype(jnp.float32) + parts[a][here].astype(jnp.float32)
            if dz == 0:
                landing[a, side, z] = total.astype(jnp.bfloat16)
                continue
            parts[a][here] = total.astype(jnp.bfloat16)
            along(a, k).start()

    def combine(a, dy, weight, put):
        for k in range(4 * dy + 1, 4 * dy + 4):
            along(a, k).wait_recv()

        def tile(columns):
            block = landing[a, dy, :, :, columns].reshape(4 * CAP, step)
            if a == 0:
                total = dot(weight[0], block, (0, 0)) + dot(weight[1], block, (0, 0))
            else:
                total = dot(weight[2], block, (0, 0))
            put(columns, total)

        tiles(tile)

    count = tokens.shape[0]
    experts = lax.broadcasted_iota(jnp.int32, (CHIPS, count), 0)
    member = [ids[c : c + 1, :] == experts for c in range(2)]
    chosen = jnp.where(member[0] | member[1], 1.0, 0.0).astype(jnp.bfloat16)
    earlier = lax.broadcasted_iota(jnp.int32, (count, count), 0) < lax.broadcasted_iota(
        jnp.int32, (count, count), 1
    )
    ranks_before = dot(chosen, jnp.where(earlier, 1.0, 0.0).astype(jnp.bfloat16), (1, 0))
    slot_of = [
        ids[c : c + 1, :] * CAP
        + jnp.sum(jnp.where(member[c], ranks_before, 0.0), axis=0, keepdims=True).astype(jnp.int32)
        for c in range(2)
    ]
    position = lax.broadcasted_iota(jnp.int32, (4 * CAP, count), 0)
    for weight, side in ((own_weight, y), (away_weight, 1 - y)):
        hits = [position + side * (4 * CAP) == slot_of[c] for c in range(2)]
        value = jnp.where(hits[0], gain[0:1, :], 0.0) + jnp.where(hits[1], gain[1:2, :], 0.0)
        high = value.astype(jnp.bfloat16)
        weight[0] = high
        weight[1] = (value - high.astype(jnp.float32)).astype(jnp.bfloat16)
        weight[2] = jnp.where(hits[0] | hits[1], 1.0, 0.0).astype(jnp.bfloat16)

    loads[0].wait()
    pl.semaphore_wait(barrier, 7)
    cross_raw(0).start()
    for placing in placings:
        placing.start()
    swap_raw.start()
    pack(0, 0)
    send(0, 0)
    loads[1].wait()
    pack(1, 0)
    send(1, 0)
    cross_raw(0).wait_send()
    cross_raw(1).start()
    placings[0].wait_recv()
    cross_raw(0).wait_recv()
    pack(0, 1)
    send(0, 1)
    receive(0, 0)
    for placing in placings[1:]:
        placing.wait_recv()
    swap_raw.wait_recv()
    mirror_pack(1)
    cross_raw(1).wait_recv()
    relay_raw.start()
    pack(1, 1)
    send(1, 1)
    receive(0, 1)
    receive(1, 0)
    settle(0, range(CHIPS))
    for load in loads[2:5]:
        load.wait()

    def units_of(i, carry):
        block = rows[0, pl.ds(i * CHIPS, CHIPS)].reshape(group, width)
        here = pl.ds(pl.multiple_of(i * group, group), group)
        for j in range(2):
            some = slice(j * half, j * half + half)
            pre_gate = dot(block, gate[:, some], (1, 0))
            pre_up = dot(block, up[:, some], (1, 0))
            pre[0, here, some] = pre_gate
            pre[1, here, some] = pre_up
            value = pre_gate * jax.nn.sigmoid(pre_gate) * pre_up
            hidden[here, some] = value.astype(jnp.bfloat16)
            factors[2, j, :, here] = value.T.astype(jnp.bfloat16)
        return carry

    lax.fori_loop(0, 2, units_of, 0)

    def grads_of(i):
        block = rows[1, pl.ds(i * CHIPS, CHIPS)].reshape(group, width)
        here = pl.ds(pl.multiple_of(i * group, group), group)
        for j in range(2):
            some = slice(j * half, j * half + half)
            hidden_grad = dot(block, down[some, :], (1, 1))
            pre_gate = pre[0, here, some]
            sigma = jax.nn.sigmoid(pre_gate)
            slope = sigma * (1.0 + pre_gate * (1.0 - sigma))
            for_gate = hidden_grad * pre[1, here, some] * slope
            for_up = hidden_grad * (pre_gate * sigma)
            gate_grad[here, some] = for_gate.astype(jnp.bfloat16)
            up_grad[here, some] = for_up.astype(jnp.bfloat16)
            factors[0, j, :, here] = for_gate.T.astype(jnp.bfloat16)
            factors[1, j, :, here] = for_up.T.astype(jnp.bfloat16)

    settle(1, range(4))
    grads_of(y)
    receive(1, 1)
    settle(1, range(4, CHIPS))
    mirror_send_on(1)
    grads_of(1 - y)
    relay_raw.wait_recv()
    for i in range(2):
        for side in range(2):
            swap(i, side).start()
    mirror_pack(0)
    mirror_send_on(0)

    def away_down(columns):
        block = rows[1, :, :, columns].reshape(2 * group, step)
        away_half[:, columns] = dot(factors[2, 1 - kept], block, (1, 0)).astype(jnp.bfloat16)

    tiles(away_down)
    swap(2, 0).start()

    def out_tile(columns):
        for i in range(2):
            part = dot(hidden[i * group : i * group + group, :], down[:, columns], (1, 0))
            out[i * CHIPS : i * CHIPS + CHIPS, :, columns] = part.astype(jnp.bfloat16).reshape(
                CHIPS, CAP, step
            )

    tiles(out_tile)
    give_halves(0)

    for a in range(2):
        for k in range(CHIPS):
            near(a, k).wait_send()
            if k % 4:
                far(a, k).wait_send()

    def input_tile(columns):
        for i in range(2):
            here = slice(i * group, i * group + group)
            part = dot(gate_grad[here, :], gate[columns, :], (1, 1))
            part += dot(up_grad[here, :], up[columns, :], (1, 1))
            slots[i * CHIPS : i * CHIPS + CHIPS, :, columns] = part.astype(jnp.bfloat16).reshape(
                CHIPS, CAP, step
            )

    add_halves(0, 1)
    tiles(input_tile)
    add_halves(0, 0)
    pl.semaphore_signal(free_sem, inc=1, device_id=(pipe, sibling), device_id_type=MESH)
    pl.semaphore_wait(free_sem, 1)
    give_halves(1)
    add_halves(1, 1)
    add_halves(1, 0)

    def own_tile(columns):
        block = rows[1, :, :, columns].reshape(2 * group, step)
        down[half:, columns] = dot(factors[2, kept], block, (1, 0)).astype(jnp.bfloat16)

    tiles(own_tile)
    results[2].start()
    mirror_receive(1)

    for a in range(2):
        if a == 0:
            cross_raw(1).wait_send()
            swap_raw.wait_send()

        def send_on(columns, total, a=a):
            mine[a, :, columns] = total.astype(jnp.bfloat16)

        combine(a, 1, relay_weight, send_on)
        across(a).start()

    mirror_receive(0)
    for k in range(CHIPS):
        mirror_near(k).wait_recv()
    loads[6].wait()
    loads[7].wait()
    loads[5].start()
    for i in range(2):
        for side in range(2):
            swap(i, side).wait_recv()
    loads[5].wait()
    targets = (grad_gate, grad_up)

    def staged(j, i):
        columns = pl.ds(pl.multiple_of(j * step, step), step)
        slot = j % 2
        return pltpu.make_async_copy(
            stage.at[slot, i], targets[i].at[columns, :], stage_sem.at[slot, i]
        )

    def weight_tile(j, carry):
        columns = pl.ds(pl.multiple_of(j * step, step), step)
        mine_rows = rows[0, :, :, columns].reshape(2 * group, step)
        their_rows = rows[1, :, :, columns].reshape(2 * group, step)
        for i in range(2):

            @pl.when(j >= 2)
            def _(i=i):
                staged(j - 2, i).wait()

            total = dot(factors[i, kept], mine_rows, (1, 0))
            total += dot(mirror_factors[i], their_rows, (1, 0))
            stage[j % 2, i] = total.T.astype(jnp.bfloat16)
            staged(j, i).start()
        return carry

    lax.fori_loop(0, 7, weight_tile, 0)

    for a in range(2):

        def keep(columns, total, a=a):
            raw[a, :, columns] = total.astype(jnp.bfloat16)

        combine(a, 0, own_weight, keep)
        results[a].start()
    swap(2, 0).wait()

    for j in (5, 6):
        for i in range(2):
            staged(j, i).wait()
    for result in results:
        result.wait()
    for i in range(2):
        for side in range(2):
            swap(i, side).wait_send()
    for placing in placings:
        placing.wait_send()
    relay_raw.wait_send()
    for a in range(2):
        across(a).wait()
        for k in range(CHIPS):
            give_half(a, k).wait_send()
            if k % 4:
                along(a, k).wait_send()
    for k in range(CHIPS):
        mirror_near(k).wait_send()
        if k % 4:
            mirror_far(k).wait_send()


def layer(tokens, grads, ids, gain, w_gate, w_up, w_down):
    count, width = tokens.shape
    units = w_gate.shape[1]
    half = units // 2
    anywhere = pl.BlockSpec(memory_space=pl.ANY)
    vmem = pl.BlockSpec(memory_space=pltpu.VMEM)
    dma = pltpu.SemaphoreType.DMA
    kind = tokens.dtype
    blocks = (2 * CHIPS, CAP, width)
    total = 2 * CHIPS * CAP
    ours = jax.ShapeDtypeStruct((count, width), kind)
    routing = pltpu.VMEM((3, total // 4, count), kind)
    weight = jax.ShapeDtypeStruct((width, half), kind)
    down = jax.ShapeDtypeStruct((half, width), kind)
    return pl.pallas_call(
        layer_kernel,
        name="layer",
        out_shape=(ours, ours, ours, ours, weight, weight, down, down, jax.ShapeDtypeStruct(blocks, kind)),
        in_specs=[anywhere] * 2 + [vmem] * 2 + [anywhere] * 3,
        out_specs=(anywhere,) * 9,
        scratch_shapes=[
            routing,
            routing,
            routing,
            pltpu.VMEM((2, total // 4, count), kind),
            pltpu.VMEM((2, count, width), kind),
            pltpu.VMEM((2, count, width), kind),
            pltpu.VMEM((2, count, width), kind),
            pltpu.VMEM(blocks, kind),
            pltpu.VMEM((CHIPS, CAP, width), kind),
            pltpu.VMEM((2, *blocks), kind),
            pltpu.VMEM(w_gate.shape, kind),
            pltpu.VMEM(w_up.shape, kind),
            pltpu.VMEM(w_down.shape, kind),
            pltpu.VMEM((2, total, units), jnp.float32),
            pltpu.VMEM((total, units), kind),
            pltpu.VMEM((total, units), kind),
            pltpu.VMEM((total, units), kind),
            pltpu.VMEM((3, 2, half, total), kind),
            pltpu.VMEM((2, half, total), kind),
            pltpu.VMEM(blocks, kind),
            pltpu.VMEM((CHIPS, CAP, width), kind),
            pltpu.VMEM((2, 2, 4, CAP, width), kind),
            pltpu.VMEM((half, width), kind),
            pltpu.VMEM((2, 2, width // 7, half), kind),
        ]
        + [dma((2, CHIPS))] * 8
        + [dma((CHIPS,))] * 4
        + [dma((2,))] * 4
        + [dma((2, 2))] * 2
        + [dma((2,))]
        + [dma((3,))] * 2
        + [dma((2,))] * 2
        + [dma((8,)), dma((2, 2)), dma((3,)), pltpu.SemaphoreType.REGULAR],
        compiler_params=pltpu.CompilerParams(
            collective_id=1, has_side_effects=True, vmem_limit_bytes=62 << 20
        ),
    )(tokens, grads, ids, gain, w_gate, w_up, w_down)[:8]


def on_device(acts, grad_out, expert_ids, route_weights, w_gate, w_up, w_down):
    tokens, grads, ids, gain = acts[0], grad_out[0], expert_ids[0], route_weights[0]
    gate_weight, up_weight, down_weight = w_gate[0], w_up[0], w_down[0]
    out_terms, input_terms, out_other, input_other, grad_gate, grad_up, own_down, other_down = layer(
        tokens, grads, ids.T, gain.T, gate_weight, up_weight, down_weight
    )

    def add(a, b):
        return (a.astype(jnp.float32) + b.astype(jnp.float32)).astype(jnp.bfloat16)[None]

    return (
        add(out_terms, out_other),
        add(input_terms, input_other),
        grad_gate[None],
        grad_up[None],
        add(own_down, other_down),
    )


def solution(mesh):
    rows = P("pipe", "expert", None)
    columns = P("pipe", None, "expert")
    return jax.shard_map(
        on_device,
        mesh=mesh,
        in_specs=(rows, rows, rows, rows, columns, columns, rows),
        out_specs=(rows, rows, columns, columns, rows),
        check_vma=False,
    )
```

```python
import functools

import jax
import jax.numpy as jnp
from jax import lax
from jax.experimental import pallas as pl
from jax.experimental.pallas import tpu as pltpu
from jax.sharding import PartitionSpec as P

MESH = pl.DeviceIdType.MESH
CHIPS = 8
CAP = 48


def place():
    pipe = lax.axis_index("pipe")
    own = lax.axis_index("expert")
    return pipe, own, own // 8, (own // 2) % 4, own % 2


def chip_at(y, z, k, sign):
    return ((y + k // 4) % 2) * 4 + (z + 4 + sign * (k % 4)) % 4


def dot(a, b, contract):
    dims = ((contract[:1], contract[1:]), ((), ()))
    return lax.dot_general(a, b, dims, preferred_element_type=jnp.float32)


def layer_kernel(
    tokens,
    grads,
    ids,
    gain,
    w_gate,
    w_up,
    w_down,
    out_terms,
    input_terms,
    out_other,
    input_other,
    grad_gate,
    grad_up,
    own_down,
    other_down,
    mirror_in,
    own_weight,
    away_weight,
    relay_weight,
    mirror_weight,
    mine,
    raw,
    mirror_raw,
    slots,
    mirror_slots,
    rows,
    gate,
    up,
    down,
    pre,
    hidden,
    gate_grad,
    up_grad,
    factors,
    mirror_factors,
    out,
    halves,
    landing,
    away_half,
    stage,
    far_send,
    far_recv,
    near_send,
    near_recv,
    half_send,
    half_recv,
    along_send,
    along_recv,
    mirror_send,
    mirror_recv,
    pass_send,
    pass_recv,
    raw_send,
    raw_recv,
    across_send,
    across_recv,
    swap_send,
    swap_recv,
    down_sem,
    away_send,
    away_recv,
    relay_send,
    relay_recv,
    load_sem,
    stage_sem,
    result_sem,
    free_sem,
):
    pipe, own, y, z, core = place()
    sibling = own + 1 - 2 * core
    opposite = (own + CHIPS) % (2 * CHIPS)
    ranks = lax.axis_size("pipe")
    mirrored = ranks - 1 - pipe
    kept = pipe // (ranks // 2)
    width = tokens.shape[1]
    units = w_gate.shape[1]
    step = width // 7
    group = CHIPS * CAP
    half = units // 2
    peers = [(y * 4 + (z + dz) % 4) * 2 + core for dz in range(4)]

    barrier = pltpu.get_barrier_semaphore()
    for peer in peers[1:] + [sibling, opposite]:
        pl.semaphore_signal(barrier, inc=1, device_id=(pipe, peer), device_id_type=MESH)
    for peer in (own, opposite):
        pl.semaphore_signal(barrier, inc=1, device_id=(mirrored, peer), device_id_type=MESH)

    loads = [
        pltpu.make_async_copy(source, target, load_sem.at[i])
        for i, (source, target) in enumerate(
            (
                (tokens, mine.at[0]),
                (grads, mine.at[1]),
                (w_gate, gate),
                (w_up, up),
                (w_down, down),
                (mirror_in, rows.at[1]),
                (mirror_slots.at[z], mirror_in.at[own]),
                (mirror_slots.at[4 + z], mirror_in.at[opposite]),
            )
        )
    ]
    for load in loads[:5]:
        load.start()

    def origin(k):
        return chip_at(y, z, k, -1) * 2 + core

    def remote(source, target, sent, got, device):
        return pltpu.make_async_remote_copy(
            src_ref=source,
            dst_ref=target,
            send_sem=sent,
            recv_sem=got,
            device_id=device,
            device_id_type=MESH,
        )

    placings = [
        remote(source, target, away_send.at[i], away_recv.at[i], device)
        for i, (source, target, device) in enumerate(
            (
                (away_weight, relay_weight, (pipe, opposite)),
                (own_weight.at[2], mirror_weight.at[0], (mirrored, own)),
                (away_weight.at[2], mirror_weight.at[1], (mirrored, opposite)),
            )
        )
    ]
    swap_raw = remote(
        mine.at[0], mirror_raw.at[1], relay_send.at[1], relay_recv.at[1], (mirrored, opposite)
    )
    relay_raw = remote(
        mirror_raw.at[1], mirror_raw.at[0], relay_send.at[0], relay_recv.at[0], (pipe, opposite)
    )

    def cross_raw(a):
        return remote(mine.at[a], raw.at[a], raw_send.at[a], raw_recv.at[a], (pipe, opposite))

    def far(a, k):
        dz = k % 4
        source = slots.at[a * 8 + (k // 4) * 4 + (z + dz) % 4]
        target = rows.at[a, (((y + k // 4) % 2) * 4 + z) * 2 + core]
        return remote(source, target, far_send.at[a, k], far_recv.at[a, k], (pipe, peers[dz]))

    def near(a, k):
        target = rows.at[a, origin(k)]
        source = target if k % 4 else slots.at[a * 8 + (k // 4) * 4 + z]
        return remote(source, target, near_send.at[a, k], near_recv.at[a, k], (pipe, sibling))

    def mirror_far(k):
        dz = k % 4
        source = mirror_slots.at[(k // 4) * 4 + (z + dz) % 4]
        target = mirror_in.at[(((y + k // 4) % 2) * 4 + z) * 2 + core]
        return remote(source, target, mirror_send.at[k], mirror_recv.at[k], (pipe, peers[dz]))

    def mirror_near(k):
        target = mirror_in.at[origin(k)]
        source = target if k % 4 else mirror_slots.at[(k // 4) * 4 + z]
        return remote(source, target, pass_send.at[k], pass_recv.at[k], (pipe, sibling))

    def swap(i, side):
        if i == 2:
            source, target = away_half, other_down
            return remote(source, target, down_sem.at[0], down_sem.at[1], (mirrored, own))
        source = factors.at[i, 1 - kept, side]
        target = mirror_factors.at[i, side]
        return remote(source, target, swap_send.at[i, side], swap_recv.at[i, side], (mirrored, own))

    parts = (out, slots)

    def give_half(a, k):
        source = parts[a].at[chip_at(y, z, k, 1) * 2 + 1 - core]
        target = halves.at[k]
        return remote(source, target, half_send.at[a, k], half_recv.at[a, k], (pipe, sibling))

    def along(a, k):
        source = parts[a].at[chip_at(y, z, k, 1) * 2 + core]
        target = landing.at[a, k // 4, z]
        device = (pipe, peers[k % 4])
        return remote(source, target, along_send.at[a, k], along_recv.at[a, k], device)

    def across(a):
        target = (out_other, input_other)[a]
        return remote(mine.at[a], target, across_send.at[a], across_recv.at[a], (pipe, opposite))

    results = [
        pltpu.make_async_copy(source, target, result_sem.at[i])
        for i, (source, target) in enumerate(
            (
                (raw.at[0], out_terms),
                (raw.at[1], input_terms),
                (down.at[pl.ds(half, half)], own_down),
            )
        )
    ]

    def tiles(body):
        def tile(j, carry):
            body(pl.ds(pl.multiple_of(j * step, step), step))
            return carry

        lax.fori_loop(0, 7, tile, 0)

    def pack(a, side):
        weight = relay_weight if side else own_weight
        source = raw if side else mine
        first = a * 8 + side * 4

        def tile(columns):
            part = source[a, :, columns]
            if a == 0:
                total = dot(weight[2], part, (1, 0))
            else:
                total = dot(weight[0], part, (1, 0)) + dot(weight[1], part, (1, 0))
            slots[first : first + 4, :, columns] = total.astype(jnp.bfloat16).reshape(4, CAP, step)

        tiles(tile)

    def send(a, side):
        for k in (2, 1, 3):
            far(a, 4 * side + k).start()
        near(a, 4 * side).start()
        rows[a, origin(4 * side)] = slots[a * 8 + side * 4 + z]

    def receive(a, side):
        for k in (1, 3, 2):
            far(a, 4 * side + k).wait_recv()
            near(a, 4 * side + k).start()

    def mirror_pack(side):
        def tile(columns):
            total = dot(mirror_weight[side], mirror_raw[side, :, columns], (1, 0))
            mirror_slots[side * 4 : side * 4 + 4, :, columns] = total.astype(jnp.bfloat16).reshape(
                4, CAP, step
            )

        tiles(tile)

    def mirror_send_on(side):
        for k in (2, 1, 3):
            mirror_far(4 * side + k).start()
        mirror_near(4 * side).start()
        loads[6 + side].start()

    def settle(a, ks):
        for k in ks:
            near(a, k).wait_recv()

    def mirror_receive(side):
        for k in (1, 3, 2):
            mirror_far(4 * side + k).wait_recv()
            mirror_near(4 * side + k).start()

    def give_halves(a, side):
        for dz in (2, 1, 3, 0):
            give_half(a, 4 * side + dz).start()

    def add_halves(a, side):
        for dz in (2, 1, 3, 0):
            k = 4 * side + dz
            here = chip_at(y, z, k, 1) * 2 + core
            give_half(a, k).wait_recv()
            total = halves[k].astype(jnp.float32) + parts[a][here].astype(jnp.float32)
            if dz == 0:
                landing[a, side, z] = total.astype(jnp.bfloat16)
                continue
            parts[a][here] = total.astype(jnp.bfloat16)
            if side == 1:
                along(a, k).start()

    def over_rows(factor, a, columns):
        total = dot(factor[0], rows[a, :CHIPS, :, columns].reshape(group, step), (1, 0))
        return total + dot(factor[1], rows[a, CHIPS:, :, columns].reshape(group, step), (1, 0))

    def combine(a, dy, weight, put):
        for k in range(4 * dy + 1, 4 * dy + 4):
            along(a, k).wait_recv()

        def tile(columns):
            block = landing[a, dy, :, :, columns].reshape(4 * CAP, step)
            if a == 0:
                total = dot(weight[0], block, (0, 0)) + dot(weight[1], block, (0, 0))
            else:
                total = dot(weight[2], block, (0, 0))
            put(columns, total)

        tiles(tile)

    count = tokens.shape[0]
    experts = lax.broadcasted_iota(jnp.int32, (CHIPS, count), 0)
    member = [ids[c : c + 1, :] == experts for c in range(2)]
    chosen = jnp.where(member[0] | member[1], 1.0, 0.0).astype(jnp.bfloat16)
    earlier = lax.broadcasted_iota(jnp.int32, (count, count), 0) < lax.broadcasted_iota(
        jnp.int32, (count, count), 1
    )
    ranks_before = dot(chosen, jnp.where(earlier, 1.0, 0.0).astype(jnp.bfloat16), (1, 0))
    slot_of = [
        ids[c : c + 1, :] * CAP
        + jnp.sum(jnp.where(member[c], ranks_before, 0.0), axis=0, keepdims=True).astype(jnp.int32)
        for c in range(2)
    ]
    position = lax.broadcasted_iota(jnp.int32, (4 * CAP, count), 0)
    for weight, side in ((own_weight, y), (away_weight, 1 - y)):
        hits = [position + side * (4 * CAP) == slot_of[c] for c in range(2)]
        value = jnp.where(hits[0], gain[0:1, :], 0.0) + jnp.where(hits[1], gain[1:2, :], 0.0)
        high = value.astype(jnp.bfloat16)
        weight[0] = high
        weight[1] = (value - high.astype(jnp.float32)).astype(jnp.bfloat16)
        weight[2] = jnp.where(hits[0] | hits[1], 1.0, 0.0).astype(jnp.bfloat16)

    loads[0].wait()
    pl.semaphore_wait(barrier, 7)
    cross_raw(0).start()
    for placing in placings:
        placing.start()
    swap_raw.start()
    pack(0, 0)
    send(0, 0)
    loads[1].wait()
    pack(1, 0)
    send(1, 0)
    cross_raw(0).wait_send()
    cross_raw(1).start()
    placings[0].wait_recv()
    cross_raw(0).wait_recv()
    pack(0, 1)
    send(0, 1)
    receive(0, 0)
    for placing in placings[1:]:
        placing.wait_recv()
    swap_raw.wait_recv()
    mirror_pack(1)
    cross_raw(1).wait_recv()
    relay_raw.start()
    pack(1, 1)
    send(1, 1)
    receive(0, 1)
    receive(1, 0)
    settle(0, range(CHIPS))
    for load in loads[2:5]:
        load.wait()

    def units_of(i, carry):
        block = rows[0, pl.ds(i * CHIPS, CHIPS)].reshape(group, width)
        here = pl.ds(pl.multiple_of(i * group, group), group)
        for j in range(2):
            some = slice(j * half, j * half + half)
            pre_gate = dot(block, gate[:, some], (1, 0))
            pre_up = dot(block, up[:, some], (1, 0))
            pre[0, here, some] = pre_gate
            pre[1, here, some] = pre_up
            value = pre_gate * jax.nn.sigmoid(pre_gate) * pre_up
            hidden[here, some] = value.astype(jnp.bfloat16)
            factors[2, j, i] = value.T.astype(jnp.bfloat16)
        return carry

    lax.fori_loop(0, 2, units_of, 0)

    def grads_of(i):
        block = rows[1, pl.ds(i * CHIPS, CHIPS)].reshape(group, width)
        here = pl.ds(pl.multiple_of(i * group, group), group)
        for j in range(2):
            some = slice(j * half, j * half + half)
            hidden_grad = dot(block, down[some, :], (1, 1))
            pre_gate = pre[0, here, some]
            sigma = jax.nn.sigmoid(pre_gate)
            slope = sigma * (1.0 + pre_gate * (1.0 - sigma))
            for_gate = hidden_grad * pre[1, here, some] * slope
            for_up = hidden_grad * (pre_gate * sigma)
            gate_grad[here, some] = for_gate.astype(jnp.bfloat16)
            up_grad[here, some] = for_up.astype(jnp.bfloat16)
            factors[0, j, i] = for_gate.T.astype(jnp.bfloat16)
            factors[1, j, i] = for_up.T.astype(jnp.bfloat16)

    settle(1, range(4))
    grads_of(y)
    receive(1, 1)
    settle(1, range(4, CHIPS))
    relay_raw.wait_recv()
    for i in range(2):
        swap(i, y).start()
    mirror_send_on(1)
    grads_of(1 - y)
    for i in range(2):
        swap(i, 1 - y).start()
    mirror_pack(0)
    mirror_send_on(0)

    def away_down(columns):
        away_half[:, columns] = over_rows(factors.at[2, 1 - kept], 1, columns).astype(jnp.bfloat16)

    tiles(away_down)
    swap(2, 0).start()

    def out_tile(columns):
        for i in range(2):
            part = dot(hidden[i * group : i * group + group, :], down[:, columns], (1, 0))
            out[i * CHIPS : i * CHIPS + CHIPS, :, columns] = part.astype(jnp.bfloat16).reshape(
                CHIPS, CAP, step
            )

    tiles(out_tile)
    give_halves(0, 1)
    give_halves(0, 0)

    def free():
        pl.semaphore_signal(free_sem, inc=1, device_id=(pipe, sibling), device_id_type=MESH)

    for a in range(2):
        for k in range(CHIPS):
            near(a, k).wait_send()
            if k % 4:
                far(a, k).wait_send()

    def input_tile(columns):
        for i in range(2):
            here = slice(i * group, i * group + group)
            part = dot(gate_grad[here, :], gate[columns, :], (1, 1))
            part += dot(up_grad[here, :], up[columns, :], (1, 1))
            slots[i * CHIPS : i * CHIPS + CHIPS, :, columns] = part.astype(jnp.bfloat16).reshape(
                CHIPS, CAP, step
            )

    add_halves(0, 1)
    free()
    tiles(input_tile)
    pl.semaphore_wait(free_sem, 1)
    give_halves(1, 1)
    add_halves(0, 0)
    free()
    pl.semaphore_wait(free_sem, 1)
    give_halves(1, 0)
    add_halves(1, 1)
    add_halves(1, 0)

    def own_tile(columns):
        down[half:, columns] = over_rows(factors.at[2, kept], 1, columns).astype(jnp.bfloat16)

    tiles(own_tile)
    results[2].start()
    mirror_receive(1)

    for a in range(2):
        if a == 0:
            cross_raw(1).wait_send()
            swap_raw.wait_send()

        def send_on(columns, total, a=a):
            mine[a, :, columns] = total.astype(jnp.bfloat16)

        combine(a, 1, relay_weight, send_on)
        across(a).start()
        if a == 0:
            for k in (5, 6, 7):
                along(1, k).wait_send()
            for b in range(2):
                for k in (1, 2, 3):
                    along(b, k).start()

    mirror_receive(0)
    for k in range(CHIPS):
        mirror_near(k).wait_recv()
    loads[6].wait()
    loads[7].wait()
    loads[5].start()
    for i in range(2):
        for side in range(2):
            swap(i, side).wait_recv()
    loads[5].wait()
    targets = (grad_gate, grad_up)

    def staged(j, i):
        columns = pl.ds(pl.multiple_of(j * step, step), step)
        slot = j % 2
        return pltpu.make_async_copy(
            stage.at[slot, i], targets[i].at[columns, :], stage_sem.at[slot, i]
        )

    def weight_tile(j, carry):
        columns = pl.ds(pl.multiple_of(j * step, step), step)
        for i in range(2):

            @pl.when(j >= 2)
            def _(i=i):
                staged(j - 2, i).wait()

            total = over_rows(factors.at[i, kept], 0, columns)
            total += over_rows(mirror_factors.at[i], 1, columns)
            stage[j % 2, i] = total.T.astype(jnp.bfloat16)
            staged(j, i).start()
        return carry

    lax.fori_loop(0, 7, weight_tile, 0)

    for a in range(2):

        def keep(columns, total, a=a):
            raw[a, :, columns] = total.astype(jnp.bfloat16)

        combine(a, 0, own_weight, keep)
        results[a].start()
    swap(2, 0).wait()

    for j in (5, 6):
        for i in range(2):
            staged(j, i).wait()
    for result in results:
        result.wait()
    for i in range(2):
        for side in range(2):
            swap(i, side).wait_send()
    for placing in placings:
        placing.wait_send()
    relay_raw.wait_send()
    for a in range(2):
        across(a).wait()
        for k in range(CHIPS):
            give_half(a, k).wait_send()
            if k % 4 and (a, k // 4) != (1, 1):
                along(a, k).wait_send()
    for k in range(CHIPS):
        mirror_near(k).wait_send()
        if k % 4:
            mirror_far(k).wait_send()


def layer(tokens, grads, ids, gain, w_gate, w_up, w_down):
    count, width = tokens.shape
    units = w_gate.shape[1]
    half = units // 2
    anywhere = pl.BlockSpec(memory_space=pl.ANY)
    vmem = pl.BlockSpec(memory_space=pltpu.VMEM)
    dma = pltpu.SemaphoreType.DMA
    kind = tokens.dtype
    blocks = (2 * CHIPS, CAP, width)
    total = 2 * CHIPS * CAP
    ours = jax.ShapeDtypeStruct((count, width), kind)
    routing = pltpu.VMEM((3, total // 4, count), kind)
    weight = jax.ShapeDtypeStruct((width, half), kind)
    down = jax.ShapeDtypeStruct((half, width), kind)
    return pl.pallas_call(
        layer_kernel,
        name="layer",
        out_shape=(ours, ours, ours, ours, weight, weight, down, down, jax.ShapeDtypeStruct(blocks, kind)),
        in_specs=[anywhere] * 2 + [vmem] * 2 + [anywhere] * 3,
        out_specs=(anywhere,) * 9,
        scratch_shapes=[
            routing,
            routing,
            routing,
            pltpu.VMEM((2, total // 4, count), kind),
            pltpu.VMEM((2, count, width), kind),
            pltpu.VMEM((2, count, width), kind),
            pltpu.VMEM((2, count, width), kind),
            pltpu.VMEM(blocks, kind),
            pltpu.VMEM((CHIPS, CAP, width), kind),
            pltpu.VMEM((2, *blocks), kind),
            pltpu.VMEM(w_gate.shape, kind),
            pltpu.VMEM(w_up.shape, kind),
            pltpu.VMEM(w_down.shape, kind),
            pltpu.VMEM((2, total, units), jnp.float32),
            pltpu.VMEM((total, units), kind),
            pltpu.VMEM((total, units), kind),
            pltpu.VMEM((total, units), kind),
            pltpu.VMEM((3, 2, 2, half, total // 2), kind),
            pltpu.VMEM((2, 2, half, total // 2), kind),
            pltpu.VMEM(blocks, kind),
            pltpu.VMEM((CHIPS, CAP, width), kind),
            pltpu.VMEM((2, 2, 4, CAP, width), kind),
            pltpu.VMEM((half, width), kind),
            pltpu.VMEM((2, 2, width // 7, half), kind),
        ]
        + [dma((2, CHIPS))] * 8
        + [dma((CHIPS,))] * 4
        + [dma((2,))] * 4
        + [dma((2, 2))] * 2
        + [dma((2,))]
        + [dma((3,))] * 2
        + [dma((2,))] * 2
        + [dma((8,)), dma((2, 2)), dma((3,)), pltpu.SemaphoreType.REGULAR],
        compiler_params=pltpu.CompilerParams(
            collective_id=1, has_side_effects=True, vmem_limit_bytes=62 << 20
        ),
    )(tokens, grads, ids, gain, w_gate, w_up, w_down)[:8]


def on_device(acts, grad_out, expert_ids, route_weights, w_gate, w_up, w_down):
    tokens, grads, ids, gain = acts[0], grad_out[0], expert_ids[0], route_weights[0]
    gate_weight, up_weight, down_weight = w_gate[0], w_up[0], w_down[0]
    out_terms, input_terms, out_other, input_other, grad_gate, grad_up, own_down, other_down = layer(
        tokens, grads, ids.T, gain.T, gate_weight, up_weight, down_weight
    )

    def add(a, b):
        return (a.astype(jnp.float32) + b.astype(jnp.float32)).astype(jnp.bfloat16)[None]

    return (
        add(out_terms, out_other),
        add(input_terms, input_other),
        grad_gate[None],
        grad_up[None],
        add(own_down, other_down),
    )


def solution(mesh):
    rows = P("pipe", "expert", None)
    columns = P("pipe", None, "expert")
    return jax.shard_map(
        on_device,
        mesh=mesh,
        in_specs=(rows, rows, rows, rows, columns, columns, rows),
        out_specs=(rows, rows, columns, columns, rows),
        check_vma=False,
    )
```

```python
import functools

import jax
import jax.numpy as jnp
from jax import lax
from jax.experimental import pallas as pl
from jax.experimental.pallas import tpu as pltpu
from jax.sharding import PartitionSpec as P

MESH = pl.DeviceIdType.MESH
CHIPS = 8
CAP = 48


def place():
    pipe = lax.axis_index("pipe")
    own = lax.axis_index("expert")
    return pipe, own, own // 8, (own // 2) % 4, own % 2


def chip_at(y, z, k, sign):
    return ((y + k // 4) % 2) * 4 + (z + 4 + sign * (k % 4)) % 4


def dot(a, b, contract):
    dims = ((contract[:1], contract[1:]), ((), ()))
    return lax.dot_general(a, b, dims, preferred_element_type=jnp.float32)


def layer_kernel(
    tokens,
    grads,
    ids,
    gain,
    w_gate,
    w_up,
    w_down,
    out_terms,
    input_terms,
    out_other,
    input_other,
    grad_gate,
    grad_up,
    own_down,
    other_down,
    mirror_in,
    own_weight,
    away_weight,
    relay_weight,
    mirror_weight,
    mine,
    raw,
    mirror_raw,
    slots,
    mirror_slots,
    rows,
    gate,
    up,
    down,
    pre,
    hidden,
    gate_grad,
    up_grad,
    factors,
    mirror_factors,
    out,
    halves,
    landing,
    away_half,
    stage,
    far_send,
    far_recv,
    near_send,
    near_recv,
    half_send,
    half_recv,
    along_send,
    along_recv,
    mirror_send,
    mirror_recv,
    pass_send,
    pass_recv,
    raw_send,
    raw_recv,
    across_send,
    across_recv,
    swap_send,
    swap_recv,
    down_sem,
    away_send,
    away_recv,
    relay_send,
    relay_recv,
    load_sem,
    stage_sem,
    result_sem,
    free_sem,
):
    pipe, own, y, z, core = place()
    sibling = own + 1 - 2 * core
    opposite = (own + CHIPS) % (2 * CHIPS)
    ranks = lax.axis_size("pipe")
    mirrored = ranks - 1 - pipe
    kept = pipe // (ranks // 2)
    width = tokens.shape[1]
    units = w_gate.shape[1]
    step = width // 7
    group = CHIPS * CAP
    half = units // 2
    peers = [(y * 4 + (z + dz) % 4) * 2 + core for dz in range(4)]

    barrier = pltpu.get_barrier_semaphore()
    for peer in peers[1:] + [sibling, opposite]:
        pl.semaphore_signal(barrier, inc=1, device_id=(pipe, peer), device_id_type=MESH)
    for peer in (own, opposite):
        pl.semaphore_signal(barrier, inc=1, device_id=(mirrored, peer), device_id_type=MESH)

    loads = [
        pltpu.make_async_copy(source, target, load_sem.at[i])
        for i, (source, target) in enumerate(
            (
                (tokens, mine.at[0]),
                (grads, mine.at[1]),
                (w_gate, gate),
                (w_up, up),
                (w_down, down),
                (mirror_in, rows.at[1]),
                (mirror_slots.at[z], mirror_in.at[own]),
                (mirror_slots.at[4 + z], mirror_in.at[opposite]),
            )
        )
    ]
    for load in loads[:2]:
        load.start()

    def origin(k):
        return chip_at(y, z, k, -1) * 2 + core

    def remote(source, target, sent, got, device):
        return pltpu.make_async_remote_copy(
            src_ref=source,
            dst_ref=target,
            send_sem=sent,
            recv_sem=got,
            device_id=device,
            device_id_type=MESH,
        )

    placings = [
        remote(source, target, away_send.at[i], away_recv.at[i], device)
        for i, (source, target, device) in enumerate(
            (
                (away_weight, relay_weight, (pipe, opposite)),
                (own_weight.at[2], mirror_weight.at[0], (mirrored, own)),
                (away_weight.at[2], mirror_weight.at[1], (mirrored, opposite)),
            )
        )
    ]
    swap_raw = remote(
        mine.at[0], mirror_raw.at[1], relay_send.at[1], relay_recv.at[1], (mirrored, opposite)
    )
    relay_raw = remote(
        mirror_raw.at[1], mirror_raw.at[0], relay_send.at[0], relay_recv.at[0], (pipe, opposite)
    )

    def cross_raw(a):
        return remote(mine.at[a], raw.at[a], raw_send.at[a], raw_recv.at[a], (pipe, opposite))

    def far(a, k):
        dz = k % 4
        source = slots.at[a * 8 + (k // 4) * 4 + (z + dz) % 4]
        target = rows.at[a, (((y + k // 4) % 2) * 4 + z) * 2 + core]
        return remote(source, target, far_send.at[a, k], far_recv.at[a, k], (pipe, peers[dz]))

    def near(a, k):
        target = rows.at[a, origin(k)]
        source = target if k % 4 else slots.at[a * 8 + (k // 4) * 4 + z]
        return remote(source, target, near_send.at[a, k], near_recv.at[a, k], (pipe, sibling))

    def mirror_far(k):
        dz = k % 4
        source = mirror_slots.at[(k // 4) * 4 + (z + dz) % 4]
        target = mirror_in.at[(((y + k // 4) % 2) * 4 + z) * 2 + core]
        return remote(source, target, mirror_send.at[k], mirror_recv.at[k], (pipe, peers[dz]))

    def mirror_near(k):
        target = mirror_in.at[origin(k)]
        source = target if k % 4 else mirror_slots.at[(k // 4) * 4 + z]
        return remote(source, target, pass_send.at[k], pass_recv.at[k], (pipe, sibling))

    def swap(i, side):
        if i == 2:
            source, target = away_half, other_down
            return remote(source, target, down_sem.at[0], down_sem.at[1], (mirrored, own))
        source = factors.at[i, 1 - kept, side]
        target = mirror_factors.at[i, side]
        return remote(source, target, swap_send.at[i, side], swap_recv.at[i, side], (mirrored, own))

    parts = (out, slots)

    def give_half(a, k):
        source = parts[a].at[chip_at(y, z, k, 1) * 2 + 1 - core]
        target = halves.at[k]
        return remote(source, target, half_send.at[a, k], half_recv.at[a, k], (pipe, sibling))

    def along(a, k):
        source = parts[a].at[chip_at(y, z, k, 1) * 2 + core]
        target = landing.at[a, k // 4, z]
        device = (pipe, peers[k % 4])
        return remote(source, target, along_send.at[a, k], along_recv.at[a, k], device)

    def across(a):
        target = (out_other, input_other)[a]
        return remote(mine.at[a], target, across_send.at[a], across_recv.at[a], (pipe, opposite))

    results = [
        pltpu.make_async_copy(source, target, result_sem.at[i])
        for i, (source, target) in enumerate(
            (
                (raw.at[0], out_terms),
                (raw.at[1], input_terms),
                (down.at[pl.ds(half, half)], own_down),
            )
        )
    ]

    def tiles(body):
        def tile(j, carry):
            body(pl.ds(pl.multiple_of(j * step, step), step))
            return carry

        lax.fori_loop(0, 7, tile, 0)

    def pack(a, side):
        weight = relay_weight if side else own_weight
        source = raw if side else mine
        first = a * 8 + side * 4

        def tile(columns):
            part = source[a, :, columns]
            if a == 0:
                total = dot(weight[2], part, (1, 0))
            else:
                total = dot(weight[0], part, (1, 0)) + dot(weight[1], part, (1, 0))
            slots[first : first + 4, :, columns] = total.astype(jnp.bfloat16).reshape(4, CAP, step)

        tiles(tile)

    def send(a, side):
        for k in (2, 1, 3):
            far(a, 4 * side + k).start()
        near(a, 4 * side).start()
        rows[a, origin(4 * side)] = slots[a * 8 + side * 4 + z]

    def receive(a, side):
        for k in (1, 3, 2):
            far(a, 4 * side + k).wait_recv()
            near(a, 4 * side + k).start()

    def mirror_pack(side):
        def tile(columns):
            total = dot(mirror_weight[side], mirror_raw[side, :, columns], (1, 0))
            mirror_slots[side * 4 : side * 4 + 4, :, columns] = total.astype(jnp.bfloat16).reshape(
                4, CAP, step
            )

        tiles(tile)

    def mirror_send_on(side):
        for k in (2, 1, 3):
            mirror_far(4 * side + k).start()
        mirror_near(4 * side).start()
        loads[6 + side].start()

    def settle(a, ks):
        for k in ks:
            near(a, k).wait_recv()

    def mirror_receive(side):
        for k in (1, 3, 2):
            mirror_far(4 * side + k).wait_recv()
            mirror_near(4 * side + k).start()

    def give_halves(a, side):
        for dz in (2, 1, 3, 0):
            give_half(a, 4 * side + dz).start()

    def add_halves(a, side):
        for dz in (2, 1, 3, 0):
            k = 4 * side + dz
            here = chip_at(y, z, k, 1) * 2 + core
            give_half(a, k).wait_recv()
            total = halves[k].astype(jnp.float32) + parts[a][here].astype(jnp.float32)
            if dz == 0:
                landing[a, side, z] = total.astype(jnp.bfloat16)
                continue
            parts[a][here] = total.astype(jnp.bfloat16)
            if side == 1:
                along(a, k).start()

    def over_rows(factor, a, columns):
        total = dot(factor[0], rows[a, :CHIPS, :, columns].reshape(group, step), (1, 0))
        return total + dot(factor[1], rows[a, CHIPS:, :, columns].reshape(group, step), (1, 0))

    def combine(a, dy, weight, put):
        for k in range(4 * dy + 1, 4 * dy + 4):
            along(a, k).wait_recv()

        def tile(columns):
            block = landing[a, dy, :, :, columns].reshape(4 * CAP, step)
            if a == 0:
                total = dot(weight[0], block, (0, 0)) + dot(weight[1], block, (0, 0))
            else:
                total = dot(weight[2], block, (0, 0))
            put(columns, total)

        tiles(tile)

    count = tokens.shape[0]
    experts = lax.broadcasted_iota(jnp.int32, (CHIPS, count), 0)
    member = [ids[c : c + 1, :] == experts for c in range(2)]
    chosen = jnp.where(member[0] | member[1], 1.0, 0.0).astype(jnp.bfloat16)
    earlier = lax.broadcasted_iota(jnp.int32, (count, count), 0) < lax.broadcasted_iota(
        jnp.int32, (count, count), 1
    )
    ranks_before = dot(chosen, jnp.where(earlier, 1.0, 0.0).astype(jnp.bfloat16), (1, 0))
    slot_of = [
        ids[c : c + 1, :] * CAP
        + jnp.sum(jnp.where(member[c], ranks_before, 0.0), axis=0, keepdims=True).astype(jnp.int32)
        for c in range(2)
    ]
    position = lax.broadcasted_iota(jnp.int32, (4 * CAP, count), 0)
    for weight, side in ((own_weight, y), (away_weight, 1 - y)):
        hits = [position + side * (4 * CAP) == slot_of[c] for c in range(2)]
        value = jnp.where(hits[0], gain[0:1, :], 0.0) + jnp.where(hits[1], gain[1:2, :], 0.0)
        high = value.astype(jnp.bfloat16)
        weight[0] = high
        weight[1] = (value - high.astype(jnp.float32)).astype(jnp.bfloat16)
        weight[2] = jnp.where(hits[0] | hits[1], 1.0, 0.0).astype(jnp.bfloat16)

    loads[0].wait()
    pl.semaphore_wait(barrier, 7)
    cross_raw(0).start()
    for placing in placings:
        placing.start()
    swap_raw.start()
    pack(0, 0)
    send(0, 0)
    loads[1].wait()
    pack(1, 0)
    send(1, 0)
    for load in loads[2:5]:
        load.start()
    cross_raw(0).wait_send()
    cross_raw(1).start()
    placings[0].wait_recv()
    cross_raw(0).wait_recv()
    pack(0, 1)
    send(0, 1)
    receive(0, 0)
    for placing in placings[1:]:
        placing.wait_recv()
    swap_raw.wait_recv()
    mirror_pack(1)
    cross_raw(1).wait_recv()
    relay_raw.start()
    pack(1, 1)
    send(1, 1)
    receive(0, 1)
    receive(1, 0)
    settle(0, range(CHIPS))
    for load in loads[2:5]:
        load.wait()

    def units_of(i, carry):
        block = rows[0, pl.ds(i * CHIPS, CHIPS)].reshape(group, width)
        here = pl.ds(pl.multiple_of(i * group, group), group)
        for j in range(2):
            some = slice(j * half, j * half + half)
            pre_gate = dot(block, gate[:, some], (1, 0))
            pre_up = dot(block, up[:, some], (1, 0))
            pre[0, here, some] = pre_gate
            pre[1, here, some] = pre_up
            value = pre_gate * jax.nn.sigmoid(pre_gate) * pre_up
            hidden[here, some] = value.astype(jnp.bfloat16)
            factors[2, j, i] = value.T.astype(jnp.bfloat16)
        return carry

    lax.fori_loop(0, 2, units_of, 0)

    def grads_of(i):
        block = rows[1, pl.ds(i * CHIPS, CHIPS)].reshape(group, width)
        here = pl.ds(pl.multiple_of(i * group, group), group)
        for j in range(2):
            some = slice(j * half, j * half + half)
            hidden_grad = dot(block, down[some, :], (1, 1))
            pre_gate = pre[0, here, some]
            sigma = jax.nn.sigmoid(pre_gate)
            slope = sigma * (1.0 + pre_gate * (1.0 - sigma))
            for_gate = hidden_grad * pre[1, here, some] * slope
            for_up = hidden_grad * (pre_gate * sigma)
            gate_grad[here, some] = for_gate.astype(jnp.bfloat16)
            up_grad[here, some] = for_up.astype(jnp.bfloat16)
            factors[0, j, i] = for_gate.T.astype(jnp.bfloat16)
            factors[1, j, i] = for_up.T.astype(jnp.bfloat16)

    settle(1, range(4))
    grads_of(y)
    receive(1, 1)
    settle(1, range(4, CHIPS))
    relay_raw.wait_recv()
    for i in range(2):
        swap(i, y).start()
    mirror_send_on(1)
    grads_of(1 - y)
    for i in range(2):
        swap(i, 1 - y).start()
    mirror_pack(0)
    mirror_send_on(0)

    def away_down(columns):
        away_half[:, columns] = over_rows(factors.at[2, 1 - kept], 1, columns).astype(jnp.bfloat16)

    tiles(away_down)
    swap(2, 0).start()

    def out_tile(columns):
        for i in range(2):
            part = dot(hidden[i * group : i * group + group, :], down[:, columns], (1, 0))
            out[i * CHIPS : i * CHIPS + CHIPS, :, columns] = part.astype(jnp.bfloat16).reshape(
                CHIPS, CAP, step
            )

    tiles(out_tile)
    give_halves(0, 1)
    give_halves(0, 0)

    def free():
        pl.semaphore_signal(free_sem, inc=1, device_id=(pipe, sibling), device_id_type=MESH)

    for a in range(2):
        for k in range(CHIPS):
            near(a, k).wait_send()
            if k % 4:
                far(a, k).wait_send()

    def input_tile(columns):
        for i in range(2):
            here = slice(i * group, i * group + group)
            part = dot(gate_grad[here, :], gate[columns, :], (1, 1))
            part += dot(up_grad[here, :], up[columns, :], (1, 1))
            slots[i * CHIPS : i * CHIPS + CHIPS, :, columns] = part.astype(jnp.bfloat16).reshape(
                CHIPS, CAP, step
            )

    add_halves(0, 1)
    free()
    tiles(input_tile)
    pl.semaphore_wait(free_sem, 1)
    give_halves(1, 1)
    add_halves(0, 0)
    free()
    pl.semaphore_wait(free_sem, 1)
    give_halves(1, 0)
    add_halves(1, 1)
    add_halves(1, 0)

    def own_tile(columns):
        down[half:, columns] = over_rows(factors.at[2, kept], 1, columns).astype(jnp.bfloat16)

    tiles(own_tile)
    results[2].start()
    mirror_receive(1)

    for a in range(2):
        if a == 0:
            cross_raw(1).wait_send()
            swap_raw.wait_send()

        def send_on(columns, total, a=a):
            mine[a, :, columns] = total.astype(jnp.bfloat16)

        combine(a, 1, relay_weight, send_on)
        across(a).start()
        if a == 0:
            for k in (5, 6, 7):
                along(1, k).wait_send()
            for b in range(2):
                for k in (1, 2, 3):
                    along(b, k).start()

    mirror_receive(0)
    for k in range(CHIPS):
        mirror_near(k).wait_recv()
    loads[6].wait()
    loads[7].wait()
    loads[5].start()
    for i in range(2):
        for side in range(2):
            swap(i, side).wait_recv()
    loads[5].wait()
    targets = (grad_gate, grad_up)

    def staged(j, i):
        columns = pl.ds(pl.multiple_of(j * step, step), step)
        slot = j % 2
        return pltpu.make_async_copy(
            stage.at[slot, i], targets[i].at[columns, :], stage_sem.at[slot, i]
        )

    def weight_tile(j, carry):
        columns = pl.ds(pl.multiple_of(j * step, step), step)
        for i in range(2):

            @pl.when(j >= 2)
            def _(i=i):
                staged(j - 2, i).wait()

            total = over_rows(factors.at[i, kept], 0, columns)
            total += over_rows(mirror_factors.at[i], 1, columns)
            stage[j % 2, i] = total.T.astype(jnp.bfloat16)
            staged(j, i).start()
        return carry

    lax.fori_loop(0, 7, weight_tile, 0)

    for a in range(2):

        def keep(columns, total, a=a):
            raw[a, :, columns] = total.astype(jnp.bfloat16)

        combine(a, 0, own_weight, keep)
        results[a].start()
    swap(2, 0).wait()

    for j in (5, 6):
        for i in range(2):
            staged(j, i).wait()
    for result in results:
        result.wait()
    for i in range(2):
        for side in range(2):
            swap(i, side).wait_send()
    for placing in placings:
        placing.wait_send()
    relay_raw.wait_send()
    for a in range(2):
        across(a).wait()
        for k in range(CHIPS):
            give_half(a, k).wait_send()
            if k % 4 and (a, k // 4) != (1, 1):
                along(a, k).wait_send()
    for k in range(CHIPS):
        mirror_near(k).wait_send()
        if k % 4:
            mirror_far(k).wait_send()


def layer(tokens, grads, ids, gain, w_gate, w_up, w_down):
    count, width = tokens.shape
    units = w_gate.shape[1]
    half = units // 2
    anywhere = pl.BlockSpec(memory_space=pl.ANY)
    vmem = pl.BlockSpec(memory_space=pltpu.VMEM)
    dma = pltpu.SemaphoreType.DMA
    kind = tokens.dtype
    blocks = (2 * CHIPS, CAP, width)
    total = 2 * CHIPS * CAP
    ours = jax.ShapeDtypeStruct((count, width), kind)
    routing = pltpu.VMEM((3, total // 4, count), kind)
    weight = jax.ShapeDtypeStruct((width, half), kind)
    down = jax.ShapeDtypeStruct((half, width), kind)
    return pl.pallas_call(
        layer_kernel,
        name="layer",
        out_shape=(ours, ours, ours, ours, weight, weight, down, down, jax.ShapeDtypeStruct(blocks, kind)),
        in_specs=[anywhere] * 2 + [vmem] * 2 + [anywhere] * 3,
        out_specs=(anywhere,) * 9,
        scratch_shapes=[
            routing,
            routing,
            routing,
            pltpu.VMEM((2, total // 4, count), kind),
            pltpu.VMEM((2, count, width), kind),
            pltpu.VMEM((2, count, width), kind),
            pltpu.VMEM((2, count, width), kind),
            pltpu.VMEM(blocks, kind),
            pltpu.VMEM((CHIPS, CAP, width), kind),
            pltpu.VMEM((2, *blocks), kind),
            pltpu.VMEM(w_gate.shape, kind),
            pltpu.VMEM(w_up.shape, kind),
            pltpu.VMEM(w_down.shape, kind),
            pltpu.VMEM((2, total, units), jnp.float32),
            pltpu.VMEM((total, units), kind),
            pltpu.VMEM((total, units), kind),
            pltpu.VMEM((total, units), kind),
            pltpu.VMEM((3, 2, 2, half, total // 2), kind),
            pltpu.VMEM((2, 2, half, total // 2), kind),
            pltpu.VMEM(blocks, kind),
            pltpu.VMEM((CHIPS, CAP, width), kind),
            pltpu.VMEM((2, 2, 4, CAP, width), kind),
            pltpu.VMEM((half, width), kind),
            pltpu.VMEM((2, 2, width // 7, half), kind),
        ]
        + [dma((2, CHIPS))] * 8
        + [dma((CHIPS,))] * 4
        + [dma((2,))] * 4
        + [dma((2, 2))] * 2
        + [dma((2,))]
        + [dma((3,))] * 2
        + [dma((2,))] * 2
        + [dma((8,)), dma((2, 2)), dma((3,)), pltpu.SemaphoreType.REGULAR],
        compiler_params=pltpu.CompilerParams(
            collective_id=1, has_side_effects=True, vmem_limit_bytes=62 << 20
        ),
    )(tokens, grads, ids, gain, w_gate, w_up, w_down)[:8]


def on_device(acts, grad_out, expert_ids, route_weights, w_gate, w_up, w_down):
    tokens, grads, ids, gain = acts[0], grad_out[0], expert_ids[0], route_weights[0]
    gate_weight, up_weight, down_weight = w_gate[0], w_up[0], w_down[0]
    out_terms, input_terms, out_other, input_other, grad_gate, grad_up, own_down, other_down = layer(
        tokens, grads, ids.T, gain.T, gate_weight, up_weight, down_weight
    )

    def add(a, b):
        return (a.astype(jnp.float32) + b.astype(jnp.float32)).astype(jnp.bfloat16)[None]

    return (
        add(out_terms, out_other),
        add(input_terms, input_other),
        grad_gate[None],
        grad_up[None],
        add(own_down, other_down),
    )


def solution(mesh):
    rows = P("pipe", "expert", None)
    columns = P("pipe", None, "expert")
    return jax.shard_map(
        on_device,
        mesh=mesh,
        in_specs=(rows, rows, rows, rows, columns, columns, rows),
        out_specs=(rows, rows, columns, columns, rows),
        check_vma=False,
    )
```
